512 devices in a mesh: dp: 32 (over z_hi, x, core), mp: 16 (over y, z_lo).
Axes of the slice: x: 4, y: 8, z: 8 (z_hi: 4, z_lo: 2; z = z_hi * 2 + z_lo), core: 2. Of those that a mesh axis runs over, the one named last changes fastest.
Arguments:
- queries: bfloat16 [10240, 6144], P('dp', 'mp'), may hold values from -4.5 to 4.5
- key_rows: bfloat16 [10240, 6144], P('dp', 'mp'), may hold values from -4.5 to 4.5
- value_rows: bfloat16 [10240, 6144], P('dp', 'mp'), may hold values from -6 to 6
- cotangent: bfloat16 [8192, 3072], P('dp'), may hold values from -6 to 6
- out_weight: bfloat16 [6144, 3072], P('mp', 'dp'), may hold values from -0.078125 to 0.078125
- patch_counts: int32 [32, 2], replicated, may hold values from 96 to 160, as said below
- destinations: int32 [32, 2], replicated, may hold values from 0 to 31, as said below
Outputs:
- attended: bfloat16 [8192, 3072], P('dp')
- grad_queries: bfloat16 [10240, 6144], P('dp', 'mp')
- grad_keys: bfloat16 [10240, 6144], P('dp', 'mp')
- grad_values: bfloat16 [10240, 6144], P('dp', 'mp')
- grad_weight: bfloat16 [6144, 3072], P('mp', 'dp')
The draws below stay inside these ranges and needn't reach their ends.
Inputs may be any that keep to these rules, and one draw needn't show every extreme that they name: `patch_counts`: every image has at most 160 patches; the images assigned to each device have exactly 256 patches in all; in every draw some device holds, in the loader's order, 2 images of 160 patches each. destinations[s, j] = (s - o_j) mod 32, with o_0 drawn afresh each run and o_1 = 31 - o_0; so each device receives one image of each index j.
All inputs are finite; a program needn't handle non-finite values.
Results may differ from the reference program's by a relative error of at most 0.022.
Values may be sent and summed in bfloat16 or wider, within the bound.
A program may use at most 64 MiB of HBM per device.

```python
import math
import jax
import jax.numpy as jnp
from jax import lax

D = 3072
HEADS = 48
HD = 128
IMGS = 2
DST_ROWS = 256
SEND = 160
SRC_TOTAL = 10240
DST_TOTAL = 8192
N_DP = 32
N_MP = 16


def images_layout(key):
    key_offsets, key_full, key_jitter = jax.random.split(key, 3)
    first = jax.random.randint(key_offsets, (), 0, N_DP, dtype=jnp.int32)
    offsets = jnp.stack([first, N_DP - 1 - first]).astype(jnp.int32)
    full_source = jax.random.randint(key_full, (), 0, N_DP, dtype=jnp.int32)
    device_ids = jnp.arange(N_DP, dtype=jnp.int32)[:, None]
    senders = (device_ids + offsets[None, :]) % N_DP
    forced = senders == full_source
    forced_any = jnp.any(forced, axis=1, keepdims=True).astype(jnp.int32)
    free_total = DST_ROWS - SEND * forced_any
    free_count = IMGS - forced_any
    base = free_total // free_count
    remainder = free_total % free_count
    spread = jnp.minimum(base - 1, SEND - base - 2)
    ranks = jnp.cumsum(jnp.logical_not(forced).astype(jnp.int32), axis=1) - 1
    ranks = jnp.maximum(ranks, 0)
    jitter = jax.random.randint(key_jitter, (N_DP, IMGS), 0, spread + 1, dtype=jnp.int32)
    following = (ranks + 1) % free_count
    lengths = base + (ranks < remainder).astype(jnp.int32) + jnp.take_along_axis(jitter, ranks, axis=1) - jnp.take_along_axis(jitter, following, axis=1)
    arriving = jnp.where(forced, SEND, lengths)
    targets = (device_ids - offsets[None, :]) % N_DP
    counts = jnp.take_along_axis(arriving, targets, axis=0)
    return (counts.astype(jnp.int32), targets.astype(jnp.int32))


def draw_patch_counts(key, part):
    counts, targets = images_layout(key)
    return counts


def draw_destinations(key, part):
    counts, targets = images_layout(key)
    return targets


def draw_queries(key, part):
    key = jax.random.fold_in(key, 5)
    shape = (N_DP * IMGS * SEND, HEADS * HD)
    values = jax.random.truncated_normal(key, -4.5, 4.5, shape, jnp.float32)
    return values.astype(jnp.bfloat16)


def draw_key_rows(key, part):
    key = jax.random.fold_in(key, 6)
    shape = (N_DP * IMGS * SEND, HEADS * HD)
    values = jax.random.truncated_normal(key, -4.5, 4.5, shape, jnp.float32)
    return values.astype(jnp.bfloat16)


def strengthened(values, rng, source, target, blocks, factor):
    def block_of(dim):
        return (jnp.arange(values.shape[dim]) // (values.shape[dim] // blocks)).reshape((-1,) + (1,) * (values.ndim - 1 - dim))

    one_side = jax.random.permutation(rng, blocks)[block_of(target)]
    second = (block_of(target) + blocks // 2) % blocks
    return jnp.where((block_of(source) == one_side) | (block_of(source) == second), factor * values, values)


def steps_of(key, dims, pieces, smallest, high):
    gain, own = 1.0, jax.random.fold_in(key, 6)
    for axis_at, shards_of in pieces:
        draws = jnp.exp(jax.random.uniform(jax.random.fold_in(own, axis_at), (shards_of,), jnp.float32, smallest / len(pieces), high / len(pieces)))
        gain = gain * jnp.repeat(draws, dims[axis_at] // shards_of).reshape([-1 if axis == axis_at else 1 for axis in range(len(dims))])
    return gain


def noise(rng, extent, scale, reach, cuts=(), held_as=jnp.bfloat16):
    values = jax.random.normal(rng, extent, jnp.float32) * scale
    if len(cuts) > 0:
        values = steps_of(rng, extent, cuts, -0.22, 0.18) * values
    return jnp.clip(values, min=-reach, max=reach).astype(held_as)


def bell_draw_with(stream_key, dims, scale, most, shards, heavy, held_as=jnp.bfloat16):
    entries = scale * jax.random.normal(stream_key, dims, jnp.float32)
    if shards:
        entries = entries * steps_of(stream_key, dims, shards, -0.22, 0.18)
    return jnp.clip(strengthened(entries, jax.random.fold_in(stream_key, 3), *heavy), -most, most).astype(held_as)


def setup_inputs(seed: int = 0) -> dict:
    splits = jax.random.split(jax.random.key(seed), 8)
    return {
        "queries": draw_queries(jax.random.fold_in(splits[7], 71), 0),
        "key_rows": draw_key_rows(jax.random.fold_in(splits[7], 71), 0),
        "value_rows": noise(splits[2], (SRC_TOTAL, HEADS * HD), 1.0, 6.0, ((0, 32), (1, 16))),
        "cotangent": bell_draw_with(splits[3], (DST_TOTAL, D), 1.0, 6.0, ((0, 32),), (0, 1, 32, 2.75)),
        "out_weight": noise(splits[4], (HEADS * HD, D), (HEADS * HD) ** -0.5, 0.078125, ((0, 16), (1, 32))),
        "patch_counts": draw_patch_counts(jax.random.fold_in(splits[7], 71), 0),
        "destinations": draw_destinations(jax.random.fold_in(splits[7], 71), 0),
    }


def layout_tables(patch_counts, destinations):
    images = patch_counts.shape[1]
    counts = patch_counts.reshape(-1)
    targets = destinations.reshape(-1)
    serial = jnp.arange(counts.shape[0], dtype=jnp.int32)
    earlier = serial[None, :] < serial[:, None]
    same_target = targets[None, :] == targets[:, None]
    same_source = serial[None, :] // images == serial[:, None] // images
    dest_start = lax.optimization_barrier(jnp.sum(jnp.where(earlier & same_target, counts[None, :], 0), axis=1)).astype(jnp.int32)
    slot_start = lax.optimization_barrier(jnp.sum(jnp.where(earlier & same_target & same_source, counts[None, :], 0), axis=1)).astype(jnp.int32)
    source_start = lax.optimization_barrier(jnp.sum(jnp.where(earlier & same_source, counts[None, :], 0), axis=1)).astype(jnp.int32)
    return (counts, targets, dest_start, slot_start, source_start)

def rounded(values):
    return lax.optimization_barrier(values.astype(jnp.bfloat16)).astype(jnp.float32)

def attention_forward(query_heads, key_heads, value_heads, segment, scale):
    highest_precision = lax.Precision.HIGHEST
    scores = jnp.einsum('rhd,shd->hrs', query_heads.astype(jnp.float32), key_heads.astype(jnp.float32), precision=highest_precision) * scale
    allowed = segment[:, None] == segment[None, :]
    scores = jnp.where(allowed[None], scores, -1e+30)
    highest = lax.optimization_barrier(jnp.max(scores, axis=-1, keepdims=True))
    weights = jnp.exp(scores - highest)
    softmaxed = weights / lax.optimization_barrier(jnp.sum(weights, axis=-1, keepdims=True))
    mixed = jnp.einsum('hrs,shd->rhd', rounded(softmaxed), value_heads.astype(jnp.float32), precision=highest_precision)
    return (mixed.astype(jnp.bfloat16), softmaxed)

def attention_backward(query_heads, key_heads, value_heads, softmaxed, grad_heads, scale):
    highest_precision = lax.Precision.HIGHEST
    grad_float = grad_heads.astype(jnp.float32)
    grad_weights = jnp.einsum('rhd,shd->hrs', grad_float, value_heads.astype(jnp.float32), precision=highest_precision)
    grad_value = jnp.einsum('hrs,rhd->shd', rounded(softmaxed), grad_float, precision=highest_precision).astype(jnp.bfloat16)
    inner = lax.optimization_barrier(jnp.sum(grad_weights * softmaxed, axis=-1, keepdims=True))
    grad_scores = rounded(softmaxed * (grad_weights - inner) * scale)
    grad_query = jnp.einsum('hrs,shd->rhd', grad_scores, key_heads.astype(jnp.float32), precision=highest_precision).astype(jnp.bfloat16)
    grad_key = jnp.einsum('hrs,rhd->shd', grad_scores, query_heads.astype(jnp.float32), precision=highest_precision).astype(jnp.bfloat16)
    return (grad_query, grad_key, grad_value)

def reference(queries, key_rows, value_rows, cotangent, out_weight, patch_counts, destinations):
    counts, targets, dest_start, slot_start, source_start = layout_tables(patch_counts, destinations)
    source_cap = IMGS * SEND
    width = HEADS * HD
    scale = 1.0 / math.sqrt(HD)
    serial = jnp.arange(N_DP * IMGS, dtype=jnp.int32)
    grouped_weight = out_weight.reshape(N_MP, width // N_MP, D).astype(jnp.float32)

    def per_device(total, device):
        row_ids = jnp.arange(DST_ROWS, dtype=jnp.int32)[:, None]
        matches = (targets[None, :] == device) & (row_ids >= dest_start[None, :]) & (row_ids < dest_start[None, :] + counts[None, :])
        position = serial[None, :] // IMGS * source_cap + source_start[None, :] + row_ids - dest_start[None, :]
        source_row = lax.optimization_barrier(jnp.sum(jnp.where(matches, position, 0), axis=1)).astype(jnp.int32)
        segment = lax.optimization_barrier(jnp.sum(jnp.where(matches, serial[None, :], 0), axis=1)).astype(jnp.int32)
        query_heads = queries[source_row].reshape(DST_ROWS, HEADS, HD)
        key_heads = key_rows[source_row].reshape(DST_ROWS, HEADS, HD)
        value_heads = value_rows[source_row].reshape(DST_ROWS, HEADS, HD)
        mixed_heads, softmaxed = attention_forward(query_heads, key_heads, value_heads, segment, scale)
        mixed_rows = mixed_heads.reshape(DST_ROWS, width)
        groups = mixed_rows.reshape(DST_ROWS, N_MP, width // N_MP).astype(jnp.float32)
        partial_value = jnp.einsum('rmc,mcd->mrd', groups, grouped_weight, precision=lax.Precision.HIGHEST)
        attended = lax.optimization_barrier(jnp.sum(rounded(partial_value), axis=0)).astype(jnp.bfloat16)
        block = lax.dynamic_slice_in_dim(cotangent, device * DST_ROWS, DST_ROWS, 0)
        grad_mixed = jnp.dot(block, out_weight.T, preferred_element_type=jnp.float32).astype(jnp.bfloat16)
        weight_term = rounded(jnp.dot(mixed_rows.T, block, preferred_element_type=jnp.float32))
        grad_query, grad_key, grad_value = attention_backward(query_heads, key_heads, value_heads, softmaxed, grad_mixed.reshape(DST_ROWS, HEADS, HD), scale)
        outputs = (attended, grad_query.reshape(DST_ROWS, width), grad_key.reshape(DST_ROWS, width), grad_value.reshape(DST_ROWS, width), source_row)
        return (total + weight_term, outputs)
    start_total = jnp.zeros((width, D), jnp.float32)
    total, stacked = lax.scan(per_device, start_total, jnp.arange(N_DP, dtype=jnp.int32))
    attended, grad_query, grad_key, grad_value, source_rows = stacked
    flat_rows = source_rows.reshape(-1)

    def restore(grads):
        empty = jnp.zeros((N_DP * source_cap, width), jnp.bfloat16)
        return empty.at[flat_rows].set(grads.reshape(-1, width))
    return (attended.reshape(N_DP * DST_ROWS, D), restore(grad_query), restore(grad_key), restore(grad_value), total.astype(jnp.bfloat16))
```

```python
import functools
import math

import jax
import jax.numpy as jnp
from jax import lax
from jax.experimental import pallas as pl
from jax.experimental.pallas import tpu as pltpu
from jax.sharding import PartitionSpec as P

HD = 128
HEADS = 3
NDP = 32
SLOT = 160
ROWS = 320
DEST = 256
FEAT = 96
WIDTH = HEADS * HD
OUT = 3072
HALF = OUT // 2
SCALE = 1.0 / math.sqrt(HD)
MESH = pl.DeviceIdType.MESH
F32 = jnp.float32
BF16 = jnp.bfloat16


def dot(a, b, dims):
    return lax.dot_general(a, b, (dims, ((), ())), preferred_element_type=F32)


def place():
    dp = lax.axis_index("dp")
    mp = lax.axis_index("mp")
    return dp, mp, dp // 8, (dp // 2) % 4, dp % 2, mp // 2, mp % 2


def dp_of(zh, x, core):
    return (zh * 4 + x) * 2 + core


def mod(a, n):
    return lax.rem(a + n, n)


def remote(src, dst, ss, rs, dp, mp):
    return pltpu.make_async_remote_copy(
        src_ref=src, dst_ref=dst, send_sem=ss, recv_sem=rs, device_id=(dp, mp), device_id_type=MESH
    )


def greet(peers):
    barrier = pltpu.get_barrier_semaphore()
    for dp, mp in peers:
        pl.semaphore_signal(barrier, inc=1, device_id=(dp, mp), device_id_type=MESH)


def greeted(count):
    pl.semaphore_wait(pltpu.get_barrier_semaphore(), count)


def tables(counts_ref, dests_ref, dp):
    o0 = mod(-dests_ref[0, 0], NDP)
    swap = (o0 >= NDP // 2).astype(jnp.int32)
    turn = jnp.where(swap == 1, NDP - 1 - o0, o0)
    c0 = counts_ref[dp, 0]
    c1 = counts_ref[dp, 1]
    home = (
        (jnp.where(swap == 1, c0, 0), jnp.where(swap == 1, c1, c0)),
        (jnp.where(swap == 1, 0, c0), jnp.where(swap == 1, c0, c1)),
    )
    src_a = lax.rem(dp + turn, NDP)
    src_b = mod(dp - turn - 1, NDP)
    count_a = counts_ref[src_a, swap]
    count_b = counts_ref[src_b, 1 - swap]
    a_first = src_a < src_b
    dest = (
        (jnp.where(a_first, 0, count_b), count_a),
        (jnp.where(a_first, count_a, 0), count_b),
    )
    return home, dest, (c0, c0 + c1)


def iota(shape, dim):
    return lax.broadcasted_iota(jnp.int32, shape, dim)


def pick(rows, start, count):
    shape = (SLOT, rows)
    r, c = iota(shape, 0), iota(shape, 1)
    return jnp.where((c == r + start) & (r < count), 1.0, 0.0).astype(BF16)


def put(rows, start, count):
    shape = (rows, SLOT)
    r, c = iota(shape, 0), iota(shape, 1)
    return jnp.where((r == c + start) & (c < count), 1.0, 0.0).astype(BF16)


def allowed(bounds):
    first, last = bounds

    def segment(shape, dim):
        ids = iota(shape, dim)
        return jnp.where(ids < first, 0, jnp.where(ids < last, 1, 2))

    return segment((ROWS, ROWS), 0) == segment((ROWS, ROWS), 1)


def probabilities(q, k, mask):
    scores = dot(q, k, ((1,), (1,))) * SCALE
    scores = jnp.where(mask, scores, -1e30)
    weights = jnp.exp(scores - jnp.max(scores, axis=-1, keepdims=True))
    return weights / jnp.sum(weights, axis=-1, keepdims=True)


def first_kernel(counts_ref, dests_ref, q_ref, k_ref, v_ref, cot_ref, w_ref, slots_ref, wt_ref, mixed_ref, ss, rs):
    dp, mp, zh, x, core, y, zl = place()
    sibling = dp_of(zh, x, 1 - core)
    xs = [dp_of(zh, lax.rem(x + i, 4), core) for i in (1, 3, 2)]
    zs = [dp_of(lax.rem(zh + i, 4), x, core) for i in (1, 3, 2)]
    peers = [sibling] + xs + zs
    greet([(p, mp) for p in peers])
    home, dest, bounds = tables(counts_ref, dests_ref, dp)
    wt_ref[dp] = jnp.transpose(w_ref[...].astype(F32)).astype(BF16)
    greeted(len(peers))
    sends = []

    def send(shard, to):
        i = len(sends)
        copy = remote(wt_ref.at[shard], wt_ref.at[shard], ss.at[i], rs.at[shard], to, mp)
        copy.start()
        sends.append(copy)

    def arrive(shard):
        remote(wt_ref.at[shard], wt_ref.at[shard], ss.at[0], rs.at[shard], dp, mp).wait_recv()

    for p in zs + xs + [sibling]:
        send(dp, p)
    mask = allowed(bounds)

    def head(h):
        cols = slice(h * HD, (h + 1) * HD)
        probs = probabilities(q_ref[:, cols], k_ref[:, cols], mask)
        mixed_ref[:, cols] = dot(probs.astype(BF16), v_ref[:, cols], ((1,), (0,))).astype(BF16)

    head(0)
    for i in (1, 3, 2):
        z = lax.rem(zh + i, 4)
        shard = dp_of(z, x, core)
        arrive(shard)
        for p in xs:
            send(shard, p)
        send(shard, sibling)
    head(1)
    for shard in xs:
        arrive(shard)
        send(shard, sibling)
    head(2)
    for slot in range(2):
        start, count = home[slot]
        slots_ref[slot] = dot(pick(ROWS, start, count), mixed_ref[...], ((1,), (0,))).astype(BF16)
    for i in (1, 3, 2):
        for j in (1, 3, 2):
            shard = dp_of(lax.rem(zh + i, 4), lax.rem(x + j, 4), core)
            arrive(shard)
            send(shard, sibling)
    for i in range(4):
        for j in range(4):
            arrive(dp_of(lax.rem(zh + i, 4), lax.rem(x + j, 4), 1 - core))
    grad = dot(cot_ref[...], wt_ref[...].reshape(OUT, WIDTH), ((1,), (0,))).astype(BF16)
    for slot in range(2):
        start, count = dest[slot]
        slots_ref[2 + slot] = dot(pick(DEST, start, count), grad, ((1,), (0,))).astype(BF16)
    for copy in sends:
        copy.wait_send()


def turn_kernel(turn, in_ref, out_ref, ss, rs):
    dp, mp, *_ = place()
    back_a, on_a = mod(dp - turn, NDP), lax.rem(dp + turn, NDP)
    on_b, back_b = lax.rem(dp + turn + 1, NDP), mod(dp - turn - 1, NDP)
    routes = [(0, back_a), (1, on_b), (2, on_a), (3, back_b)]
    if turn == 0:
        others = [routes[1], routes[3]]
        own = [routes[0], routes[2]]
    else:
        others, own = routes, []
    greet([(p, mp) for _, p in others])
    local = [pltpu.make_async_copy(in_ref.at[i], out_ref.at[i], ss.at[i]) for i, _ in own]
    for copy in local:
        copy.start()
    greeted(len(others))
    copies = [remote(in_ref.at[i], out_ref.at[i], ss.at[i], rs.at[i], p, mp) for i, p in others]
    for copy in copies:
        copy.start()
    for copy in local + copies:
        copy.wait()


def second_kernel(
    counts_ref, dests_ref, in_ref, q_ref, k_ref, v_ref, cot_ref, wt_ref,
    att_ref, gq_ref, gk_ref, gv_ref, gw_ref,
    mixed_ref, part_ref, ring_ref, fold_ref, term_ref, core_ref, xin_ref, zin_ref, gm_ref,
    ring_s, ring_r, fold_s, fold_r, gath_s, gath_r, red_s, red_r,
):
    dp, mp, zh, x, core, y, zl = place()
    mp_of = lambda yy, zz: yy * 2 + zz
    up, down = mp_of(lax.rem(y + 1, 8), zl), mp_of(lax.rem(y + 7, 8), zl)
    across = mp_of(y, 1 - zl)
    sibling = dp_of(zh, x, 1 - core)
    xs = [dp_of(zh, lax.rem(x + i, 4), core) for i in (1, 3, 2)]
    zs = [dp_of(lax.rem(zh + i, 4), x, core) for i in (1, 3, 2)]
    greet([(dp, up), (dp, down), (dp, across)] + [(p, mp) for p in [sibling] + xs + zs])
    home, dest, bounds = tables(counts_ref, dests_ref, dp)
    mixed_ref[...] = (
        dot(put(DEST, *dest[0]), in_ref[0], ((1,), (0,))) + dot(put(DEST, *dest[1]), in_ref[1], ((1,), (0,)))
    ).astype(BF16)
    for c in range(8):
        cols = slice(c * WIDTH, (c + 1) * WIDTH)
        w = wt_ref[4 * c : 4 * c + 4].reshape(WIDTH, WIDTH)
        part_ref[:, cols] = dot(mixed_ref[...], w, ((1,), (1,))).astype(BF16)
    greeted(10)

    def chunk(ref, yy, sub):
        rows = pl.ds(pl.multiple_of(yy * 32, 32), 32)
        return ref.at[rows, pl.ds(sub * HALF, HALF)]

    pending = []

    def ring_copy(way, step, sub):
        to = up if way == 0 else down
        yy = lax.rem(y + 4 - step, 8) if way == 0 else lax.rem(y + 4 + step, 8)
        return remote(
            chunk(part_ref, yy, sub), ring_ref.at[way, step, sub], ring_s.at[way, step, sub],
            ring_r.at[way, step, sub], dp, to,
        )

    def ring_send(way, step, sub):
        copy = ring_copy(way, step, sub)
        copy.start()
        pending.append(copy)

    def ring_take(way, step, sub):
        ring_copy(way, step, sub).wait_recv()
        yy = lax.rem(y + 3 - step, 8) if way == 0 else lax.rem(y + 5 + step, 8)
        ref = chunk(part_ref, yy, sub)
        ref[...] = (ref[...].astype(F32) + ring_ref[way, step, sub].astype(F32)).astype(BF16)

    ring_send(0, 0, 0)
    ring_send(1, 0, 1)
    ring_send(0, 1, 1)
    ring_send(1, 1, 0)

    for c in range(8):
        cols = slice(c * WIDTH, (c + 1) * WIDTH)
        block = dot(cot_ref[:, cols], mixed_ref[...], ((0,), (0,))).astype(BF16)
        for i in range(4):
            j = 4 * c + i
            term_ref[j % 2, (j // 2) % 4, j // 8] = block[i * FEAT : (i + 1) * FEAT]
    swap = remote(term_ref.at[1 - core], core_ref, red_s.at[0], red_r.at[0], sibling, mp)
    swap.start()

    ring_take(0, 0, 0)
    ring_send(0, 1, 0)
    ring_take(1, 0, 1)
    ring_send(1, 1, 1)

    swap.wait_recv()
    term_ref[core] = (term_ref[core].astype(F32) + core_ref[...].astype(F32)).astype(BF16)
    xcopies = []
    for n, i in enumerate((1, 3, 2)):
        copy = remote(
            term_ref.at[core, lax.rem(x + i, 4)], xin_ref.at[n], red_s.at[1 + n], red_r.at[1 + n], xs[n], mp
        )
        copy.start()
        xcopies.append(copy)

    for step in (1, 2):
        for way, sub in ((0, 1), (1, 0), (0, 0), (1, 1)):
            ring_take(way, step, sub)
            ring_send(way, step + 1, sub)

    for copy in xcopies:
        copy.wait_recv()
    total = term_ref[core, x].astype(F32)
    for n in range(3):
        total = total + xin_ref[n].astype(F32)
    term_ref[core, x] = total.astype(BF16)
    zcopies = []
    for n, i in enumerate((1, 3, 2)):
        copy = remote(
            term_ref.at[core, x, lax.rem(zh + i, 4)], zin_ref.at[n], red_s.at[4 + n], red_r.at[4 + n], zs[n], mp
        )
        copy.start()
        zcopies.append(copy)

    folds = []
    for way, sub in ((0, 1), (0, 0)):
        other = 1 - way
        ring_copy(way, 3, sub).wait_recv()
        ring_copy(other, 3, sub).wait_recv()
        ref = chunk(part_ref, y, sub)
        ref[...] = (
            ref[...].astype(F32) + ring_ref[way, 3, sub].astype(F32) + ring_ref[other, 3, sub].astype(F32)
        ).astype(BF16)
        copy = remote(ref, fold_ref.at[sub], fold_s.at[sub], fold_r.at[sub], dp, across)
        copy.start()
        folds.append((sub, copy))

    def gather_copy(way, step, sub):
        to = up if way == 0 else down
        yy = mod(y - step, 8) if way == 0 else lax.rem(y + step, 8)
        return remote(
            chunk(att_ref, yy, sub), chunk(att_ref, yy, sub), gath_s.at[way, step, sub],
            gath_r.at[way, step, sub], dp, to,
        )

    def gather_send(way, step, sub):
        copy = gather_copy(way, step, sub)
        copy.start()
        pending.append(copy)

    def gather_take(way, step, sub):
        to = up if way == 0 else down
        yy = mod(y - step - 1, 8) if way == 0 else lax.rem(y + step + 1, 8)
        remote(
            chunk(att_ref, yy, sub), chunk(att_ref, yy, sub), gath_s.at[way, step, sub],
            gath_r.at[way, step, sub], dp, to,
        ).wait_recv()

    for sub, copy in folds:
        copy.wait_recv()
        mine = chunk(part_ref, y, sub)
        chunk(att_ref, y, sub)[...] = (mine[...].astype(F32) + fold_ref[sub].astype(F32)).astype(BF16)
        gather_send(0, 0, sub)
        gather_send(1, 0, sub)

    gm_ref[...] = (
        dot(put(ROWS, *home[0]), in_ref[2], ((1,), (0,))) + dot(put(ROWS, *home[1]), in_ref[3], ((1,), (0,)))
    ).astype(BF16)
    mask = allowed(bounds)

    def head(h):
        cols = slice(h * HD, (h + 1) * HD)
        q, k, v, gm = q_ref[:, cols], k_ref[:, cols], v_ref[:, cols], gm_ref[:, cols]
        probs = probabilities(q, k, mask)
        gp = dot(gm, v, ((1,), (1,)))
        gv_ref[:, cols] = dot(probs.astype(BF16), gm, ((0,), (0,))).astype(BF16)
        inner = jnp.sum(gp * probs, axis=-1, keepdims=True)
        gs = (probs * (gp - inner) * SCALE).astype(BF16)
        gq_ref[:, cols] = dot(gs, k, ((1,), (0,))).astype(BF16)
        gk_ref[:, cols] = dot(gs, q, ((0,), (0,))).astype(BF16)

    for step in range(2):
        head(step)
        for way, sub in ((0, 1), (1, 1), (0, 0), (1, 0)):
            gather_take(way, step, sub)
            gather_send(way, step + 1, sub)
    head(2)
    for way, sub in ((0, 1), (1, 1), (0, 0), (1, 0)):
        gather_take(way, 2, sub)
        if way == sub:
            gather_send(way, 3, sub)
    for copy in zcopies:
        copy.wait_recv()
    total = term_ref[core, x, zh].astype(F32)
    for n in range(3):
        total = total + zin_ref[n].astype(F32)
    gw_ref[...] = jnp.transpose(total).astype(BF16)
    gather_take(0, 3, 0)
    gather_take(1, 3, 1)
    for copy in pending + [swap] + xcopies + zcopies + [c for _, c in folds]:
        copy.wait_send()


def vmem():
    return pl.BlockSpec(memory_space=pltpu.VMEM)


def smem():
    return pl.BlockSpec(memory_space=pltpu.SMEM)


def params(cid):
    return pltpu.CompilerParams(collective_id=cid, has_side_effects=True, vmem_limit_bytes=48 << 20)


def sds(*shape):
    return jax.ShapeDtypeStruct(shape, BF16)


DMA = pltpu.SemaphoreType.DMA


def local(queries, key_rows, value_rows, cotangent, out_weight, patch_counts, destinations):
    slots, wt = pl.pallas_call(
        first_kernel,
        out_shape=(sds(4, SLOT, WIDTH), sds(NDP, FEAT, WIDTH)),
        in_specs=[smem(), smem()] + [vmem()] * 5,
        out_specs=(vmem(), vmem()),
        scratch_shapes=[pltpu.VMEM((ROWS, WIDTH), BF16), DMA((31,)), DMA((32,))],
        compiler_params=params(0),
        name="gather_forward",
    )(patch_counts, destinations, queries, key_rows, value_rows, cotangent, out_weight)

    def turner(turn):
        return pl.pallas_call(
            functools.partial(turn_kernel, turn),
            out_shape=sds(4, SLOT, WIDTH),
            in_specs=[vmem()],
            out_specs=vmem(),
            scratch_shapes=[DMA((4,)), DMA((4,))],
            compiler_params=params(2 + turn),
            name="turn_%d" % turn,
        )

    first = jnp.mod(-destinations[0, 0], NDP)
    index = jnp.where(first >= NDP // 2, NDP - 1 - first, first)
    turned = lax.switch(index, [turner(t) for t in range(NDP // 2)], slots)

    return pl.pallas_call(
        second_kernel,
        out_shape=(sds(DEST, OUT), sds(ROWS, WIDTH), sds(ROWS, WIDTH), sds(ROWS, WIDTH), sds(WIDTH, FEAT)),
        in_specs=[smem(), smem()] + [vmem()] * 6,
        out_specs=(vmem(),) * 5,
        scratch_shapes=[
            pltpu.VMEM((DEST, WIDTH), BF16),
            pltpu.VMEM((DEST, OUT), BF16),
            pltpu.VMEM((2, 4, 2, 32, HALF), BF16),
            pltpu.VMEM((2, 32, HALF), BF16),
            pltpu.VMEM((2, 4, 4, FEAT, WIDTH), BF16),
            pltpu.VMEM((4, 4, FEAT, WIDTH), BF16),
            pltpu.VMEM((3, 4, FEAT, WIDTH), BF16),
            pltpu.VMEM((3, FEAT, WIDTH), BF16),
            pltpu.VMEM((ROWS, WIDTH), BF16),
            DMA((2, 4, 2)), DMA((2, 4, 2)),
            DMA((2,)), DMA((2,)),
            DMA((2, 4, 2)), DMA((2, 4, 2)),
            DMA((7,)), DMA((7,)),
        ],
        compiler_params=params(1),
        name="project_backward",
    )(patch_counts, destinations, turned, queries, key_rows, value_rows, cotangent, wt)


def solution(mesh):
    in_specs = (P("dp", "mp"), P("dp", "mp"), P("dp", "mp"), P("dp", None), P("mp", "dp"), P(), P())
    out_specs = (P("dp", None), P("dp", "mp"), P("dp", "mp"), P("dp", "mp"), P("mp", "dp"))
    return jax.shard_map(local, mesh=mesh, in_specs=in_specs, out_specs=out_specs, check_vma=False)
```

```python
import functools
import math

import jax
import jax.numpy as jnp
from jax import lax
from jax.experimental import pallas as pl
from jax.experimental.pallas import tpu as pltpu
from jax.sharding import PartitionSpec as P

HD = 128
HEADS = 3
NDP = 32
SLOT = 160
ROWS = 320
DEST = 256
FEAT = 96
WIDTH = HEADS * HD
OUT = 3072
SUB = DEST // 2
SCALE = 1.0 / math.sqrt(HD)
MESH = pl.DeviceIdType.MESH
F32 = jnp.float32
BF16 = jnp.bfloat16


def dot(a, b, dims):
    return lax.dot_general(a, b, (dims, ((), ())), preferred_element_type=F32)


def place():
    dp = lax.axis_index("dp")
    mp = lax.axis_index("mp")
    return dp, mp, dp // 8, (dp // 2) % 4, dp % 2, mp // 2, mp % 2


def block(i, size):
    return pl.ds(pl.multiple_of(i * size, size), size)


def near(i):
    return 2 * i + 1 - 3 * (i // 2)


def jump(i):
    return i + (i + 1) // 3 - 2 * (i // 3)


def dp_of(zh, x, core):
    return (zh * 4 + x) * 2 + core


def mod(a, n):
    return lax.rem(a + n, n)


def remote(src, dst, ss, rs, dp, mp):
    return pltpu.make_async_remote_copy(
        src_ref=src, dst_ref=dst, send_sem=ss, recv_sem=rs, device_id=(dp, mp), device_id_type=MESH
    )


def greet(peers):
    barrier = pltpu.get_barrier_semaphore()
    for dp, mp in peers:
        pl.semaphore_signal(barrier, inc=1, device_id=(dp, mp), device_id_type=MESH)


def greeted(count):
    pl.semaphore_wait(pltpu.get_barrier_semaphore(), count)


def tables(turn, counts_ref, dests_ref, dp):
    swap = (mod(-dests_ref[0, 0], NDP) >= NDP // 2).astype(jnp.int32)
    c0 = counts_ref[0, dp]
    c1 = counts_ref[1, dp]
    home = (
        (jnp.where(swap == 1, c0, 0), jnp.where(swap == 1, c1, c0)),
        (jnp.where(swap == 1, 0, c0), jnp.where(swap == 1, c0, c1)),
    )
    src_a = lax.rem(dp + turn, NDP)
    src_b = mod(dp - turn - 1, NDP)
    count_a = counts_ref[swap, src_a]
    count_b = counts_ref[1 - swap, src_b]
    a_first = src_a < src_b
    dest = (
        (jnp.where(a_first, 0, count_b), count_a),
        (jnp.where(a_first, count_a, 0), count_b),
    )
    return home, dest, (c0, c0 + c1)


def iota(shape, dim):
    return lax.broadcasted_iota(jnp.int32, shape, dim)


def pick(rows, start, count):
    shape = (SLOT, rows)
    r, c = iota(shape, 0), iota(shape, 1)
    return jnp.where((c == r + start) & (r < count), 1.0, 0.0).astype(BF16)


def put(rows, start, count):
    shape = (rows, SLOT)
    r, c = iota(shape, 0), iota(shape, 1)
    return jnp.where((r == c + start) & (c < count), 1.0, 0.0).astype(BF16)


def allowed(bounds):
    first, last = bounds

    def segment(shape, dim):
        ids = iota(shape, dim)
        return jnp.where(ids < first, 0, jnp.where(ids < last, 1, 2))

    return segment((ROWS, ROWS), 0) == segment((ROWS, ROWS), 1)


def probabilities(q, k, mask):
    scores = dot(q, k, ((1,), (1,))) * SCALE
    scores = jnp.where(mask, scores, -1e30)
    weights = jnp.exp(scores - jnp.max(scores, axis=-1, keepdims=True))
    return weights / jnp.sum(weights, axis=-1, keepdims=True)


def fused(
    turn, counts_ref, dests_ref, q_hbm, k_hbm, v_hbm, cot_hbm, w_hbm,
    att_hbm, gq_hbm, gk_hbm, gv_hbm, gw_hbm,
    qkv_ref, cot_ref, wt_ref, mixed_ref, slots_ref, turned_ref, dest_ref, gm_ref, part_ref, ring_ref, fold_ref,
    att_ref, term_ref, core_ref, xin_ref, zin_ref, grads_ref, gw_ref, sum_ref,
    load, store, att_store, wt_s, wt_r, turn_s, turn_r, ring_s, ring_r, fold_s, fold_r, gath_s, gath_r, red_s, red_r,
):
    dp, mp, zh, x, core, y, zl = place()
    up, down = lax.rem(y + 1, 8) * 2 + zl, lax.rem(y + 7, 8) * 2 + zl
    across = y * 2 + 1 - zl
    sibling = dp_of(zh, x, 1 - core)
    xs = [dp_of(zh, lax.rem(x + i, 4), core) for i in (1, 3, 2)]
    zs = [dp_of(lax.rem(zh + i, 4), x, core) for i in (1, 3, 2)]
    back_a, on_a = mod(dp - turn, NDP), lax.rem(dp + turn, NDP)
    on_b, back_b = lax.rem(dp + turn + 1, NDP), mod(dp - turn - 1, NDP)
    routes = [back_a, on_b, on_a, back_b]
    peers = [(dp, up), (dp, down), (dp, across)] + [(p, mp) for p in [sibling] + xs + zs]
    peers += [(routes[i], mp) for i in range(4) if turn or i % 2]
    greet(peers)

    loads = [pltpu.make_async_copy(w_hbm, wt_ref.at[dp], load.at[0])]
    for i, ref in enumerate((q_hbm, k_hbm, v_hbm)):
        loads.append(pltpu.make_async_copy(ref, qkv_ref.at[i], load.at[1 + i]))
    loads.append(pltpu.make_async_copy(cot_hbm, cot_ref, load.at[4]))
    for copy in loads:
        copy.start()
    home, dest, bounds = tables(turn, counts_ref, dests_ref, dp)
    pending = []

    def shard_send(i, shard, to):
        remote(wt_ref.at[shard], wt_ref.at[shard], wt_s.at[i], wt_r.at[shard], to, mp).start()

    def shard_wait(shard):
        remote(wt_ref.at[shard], wt_ref.at[shard], wt_s.at[0], wt_r.at[shard], dp, mp).wait_recv()

    loads[0].wait()
    greeted(len(peers))
    for i, p in enumerate(zs + xs + [sibling]):
        shard_send(i, dp, p)

    for copy in loads[1:4]:
        copy.wait()
    @pl.loop(0, HEADS)
    def _(h):
        cols = block(h, HD)
        probs = probabilities(qkv_ref[0, :, cols], qkv_ref[1, :, cols], allowed(bounds))
        mixed_ref[:, cols] = dot(probs.astype(BF16), qkv_ref[2, :, cols], ((1,), (0,))).astype(BF16)

    def turn_copy(i):
        if turn == 0 and i % 2 == 0:
            return pltpu.make_async_copy(slots_ref.at[i], turned_ref.at[i], turn_s.at[i])
        return remote(slots_ref.at[i], turned_ref.at[i], turn_s.at[i], turn_r.at[i], routes[i], mp)

    turns = [turn_copy(i) for i in range(4)]

    def turn_wait(i):
        if turn == 0 and i % 2 == 0:
            turns[i].wait()
        else:
            turns[i].wait_recv()
            pending.append(turns[i])

    def either(slot, pair):
        return [jnp.where(slot == 0, a, b) for a, b in zip(*pair)]

    @pl.loop(0, 2)
    def _(slot):
        slots_ref[slot] = dot(pick(ROWS, *either(slot, home)), mixed_ref[...], ((1,), (0,))).astype(BF16)

    for slot in range(2):
        turns[slot].start()

    def place_rows(ref, first, spans):
        @pl.loop(0, ref.shape[0] // 64)
        def _(i):
            rows = 0.0
            for n, (start, count) in enumerate(spans):
                rows = rows + dot(put(64, start - 64 * i, count), turned_ref[first + n], ((1,), (0,)))
            ref[block(i, 64)] = rows.astype(BF16)

    @pl.loop(0, 3)
    def _(i):
        shard = dp_of(lax.rem(zh + near(i), 4), x, core)
        shard_wait(shard)
        for j, p in enumerate(xs + [sibling]):
            shard_send(7 + 4 * i + j, shard, p)

    @pl.loop(0, 12)
    def _(i):
        shard = dp_of(lax.rem(zh + jump(i // 3), 4), lax.rem(x + near(lax.rem(i, 3)), 4), core)
        shard_wait(shard)
        shard_send(19 + i, shard, sibling)

    for slot in range(2):
        turn_wait(slot)
    place_rows(dest_ref, 0, dest)
    loads[4].wait()

    @pl.loop(0, 16)
    def _(i):
        shard_wait(2 * i + 1 - core)

    @pl.loop(0, 31)
    def _(i):
        remote(wt_ref.at[dp], wt_ref.at[dp], wt_s.at[i], wt_r.at[dp], sibling, mp).wait_send()

    def ring_copy(way, step, sub):
        to = up if way == 0 else down
        yy = lax.rem(y + 4 - step, 8) if way == 0 else lax.rem(y + 4 + step, 8)
        return remote(
            part_ref.at[yy, sub], ring_ref.at[way, step, sub], ring_s.at[way, step, sub], ring_r.at[way, step, sub],
            dp, to,
        )

    def ring_send(way, step, sub):
        ring_copy(way, step, sub).start()

    def add(out, *refs):
        @pl.loop(0, out.shape[0] // 32)
        def _(i):
            total = 0.0
            for ref in refs:
                total = total + ref[block(i, 32)].astype(F32)
            out[block(i, 32)] = total.astype(BF16)

    def ring_take(way, step, sub):
        ring_copy(way, step, sub).wait_recv()
        yy = lax.rem(y + 3 - step, 8) if way == 0 else lax.rem(y + 5 + step, 8)
        add(part_ref.at[yy, sub], part_ref.at[yy, sub], ring_ref.at[way, step, sub])

    @pl.loop(0, 8)
    def _(c):
        w = wt_ref[pl.ds(4 * c, 4)].reshape(WIDTH, WIDTH)
        part_ref[c] = dot(dest_ref[...], w, ((1,), (1,))).astype(BF16).reshape(2, SUB, WIDTH)

    ring_send(0, 0, 0)
    ring_send(1, 0, 1)
    ring_send(0, 1, 1)
    ring_send(1, 1, 0)

    sum_ref[...] = jnp.zeros_like(sum_ref)

    @pl.loop(0, 8)
    def _(c):
        w = wt_ref[pl.ds(4 * c, 4)].reshape(WIDTH, WIDTH)
        sum_ref[...] += dot(cot_ref[:, block(c, WIDTH)], w, ((1,), (0,)))

    @pl.loop(0, 2)
    def _(slot):
        picked = pick(DEST, *either(slot, dest))
        slots_ref[2 + slot] = dot(picked, sum_ref[...].astype(BF16), ((1,), (0,))).astype(BF16)

    for slot in range(2):
        turns[2 + slot].start()

    @pl.loop(0, 8)
    def _(c):
        term = dot(cot_ref[:, block(c, WIDTH)], dest_ref[...], ((0,), (0,))).astype(BF16)
        for i in range(4):
            term_ref[i % 2, lax.rem(2 * c + i // 2, 4), c // 2] = term[i * FEAT : (i + 1) * FEAT]

    swap = remote(term_ref.at[1 - core], core_ref, red_s.at[0], red_r.at[0], sibling, mp)
    swap.start()
    pending.append(swap)

    for way, sub in ((0, 0), (1, 1)):
        ring_take(way, 0, sub)
        ring_send(way, 1, sub)

    swap.wait_recv()
    @pl.loop(0, 16)
    def _(i):
        ref = term_ref.at[core, i // 4, lax.rem(i, 4)]
        add(ref, ref, core_ref.at[i // 4, lax.rem(i, 4)])

    xcopies = []
    for n, i in enumerate((1, 3, 2)):
        copy = remote(term_ref.at[core, lax.rem(x + i, 4)], xin_ref.at[n], red_s.at[1 + n], red_r.at[1 + n], xs[n], mp)
        copy.start()
        xcopies.append(copy)
    pending.extend(xcopies)

    @pl.loop(1, 3)
    def _(step):
        for way, sub in ((0, 1), (1, 0), (0, 0), (1, 1)):
            ring_take(way, step, sub)
            ring_send(way, step + 1, sub)

    folds = []
    for sub in (1, 0):
        for way in range(2):
            ring_copy(way, 3, sub).wait_recv()
        add(part_ref.at[y, sub], part_ref.at[y, sub], ring_ref.at[0, 3, sub], ring_ref.at[1, 3, sub])
        copy = remote(part_ref.at[y, sub], fold_ref.at[sub], fold_s.at[sub], fold_r.at[sub], dp, across)
        copy.start()
        folds.append((sub, copy))
        pending.append(copy)

    for copy in xcopies:
        copy.wait_recv()
    @pl.loop(0, 4)
    def _(i):
        add(term_ref.at[core, x, i], term_ref.at[core, x, i], *[xin_ref.at[n, i] for n in range(3)])

    zcopies = []
    for n, i in enumerate((1, 3, 2)):
        copy = remote(
            term_ref.at[core, x, lax.rem(zh + i, 4)], zin_ref.at[n], red_s.at[4 + n], red_r.at[4 + n], zs[n], mp
        )
        copy.start()
        zcopies.append(copy)
    pending.extend(zcopies)

    def att_copy(i, yy, sub):
        rows, cols = pl.ds(sub * SUB, SUB), block(yy, WIDTH)
        return pltpu.make_async_copy(att_ref.at[yy, sub], att_hbm.at[rows, cols], att_store.at[i])

    def gather_copy(way, step, sub, yy):
        to = up if way == 0 else down
        return remote(
            att_ref.at[yy, sub], att_ref.at[yy, sub], gath_s.at[way, step, sub], gath_r.at[way, step, sub], dp, to
        )

    def gather_send(way, step, sub):
        gather_copy(way, step, sub, mod(y - step, 8) if way == 0 else lax.rem(y + step, 8)).start()

    def gather_take(way, step, sub):
        yy = mod(y - step - 1, 8) if way == 0 else lax.rem(y + step + 1, 8)
        gather_copy(way, step, sub, yy).wait_recv()
        att_copy(2 + 4 * step + 2 * way + sub if not isinstance(step, int) or step < 3 else 14 + way, yy, sub).start()

    for sub, copy in folds:
        copy.wait_recv()
        add(att_ref.at[y, sub], part_ref.at[y, sub], fold_ref.at[sub])
        gather_send(0, 0, sub)
        gather_send(1, 0, sub)
        att_copy(sub, y, sub).start()

    for slot in range(2):
        turn_wait(2 + slot)
    place_rows(gm_ref, 2, home)

    @pl.loop(0, HEADS)
    def _(h):
        cols = block(h, HD)
        q, k, v, gm = qkv_ref[0, :, cols], qkv_ref[1, :, cols], qkv_ref[2, :, cols], gm_ref[:, cols]
        probs = probabilities(q, k, allowed(bounds))
        gp = dot(gm, v, ((1,), (1,)))
        grads_ref[2, :, cols] = dot(probs.astype(BF16), gm, ((0,), (0,))).astype(BF16)
        inner = jnp.sum(gp * probs, axis=-1, keepdims=True)
        gs = (probs * (gp - inner) * SCALE).astype(BF16)
        grads_ref[0, :, cols] = dot(gs, k, ((1,), (0,))).astype(BF16)
        grads_ref[1, :, cols] = dot(gs, q, ((0,), (0,))).astype(BF16)

    outs = []
    @pl.loop(0, 2)
    def _(step):
        for way, sub in ((0, 1), (1, 1), (0, 0), (1, 0)):
            gather_take(way, step, sub)
            gather_send(way, step + 1, sub)

    for way, sub in ((1, 1), (0, 0), (0, 1), (1, 0)):
        gather_take(way, 2, sub)
        if way == sub:
            gather_send(way, 3, sub)
    for i, ref in enumerate((gq_hbm, gk_hbm, gv_hbm)):
        outs.append(pltpu.make_async_copy(grads_ref.at[i], ref, store.at[i]))
    for copy in zcopies:
        copy.wait_recv()
    add(gw_ref, term_ref.at[core, x, zh], *[zin_ref.at[n] for n in range(3)])
    outs.append(pltpu.make_async_copy(gw_ref, gw_hbm, store.at[3]))
    for copy in outs:
        copy.start()
    for way in range(2):
        gather_take(way, 3, way)
    for copy in outs:
        copy.wait()

    @pl.loop(0, 16)
    def _(i):
        att_copy(i, 0, 0).wait()

    def sent(way, step, sub):
        ring_copy(way, step, sub).wait_send()
        gather_copy(way, step, sub, y).wait_send()

    @pl.loop(1, 3)
    def _(step):
        for way in range(2):
            for sub in range(2):
                sent(way, step, sub)

    for way in range(2):
        sent(way, 0, way)
        sent(way, 3, way)
        ring_copy(way, 3, 1 - way).wait_send()
        gather_copy(way, 0, 1 - way, y).wait_send()
    for copy in pending:
        copy.wait_send()


def sds(*shape):
    return jax.ShapeDtypeStruct(shape, BF16)


def buf(*shape):
    return pltpu.VMEM(shape, BF16)


DMA = pltpu.SemaphoreType.DMA


def local(queries, key_rows, value_rows, cotangent, out_weight, patch_counts, destinations):
    def branch(turn):
        smem, hbm = pl.BlockSpec(memory_space=pltpu.SMEM), pl.BlockSpec(memory_space=pl.ANY)
        return pl.pallas_call(
            functools.partial(fused, turn),
            out_shape=(sds(DEST, OUT), sds(ROWS, WIDTH), sds(ROWS, WIDTH), sds(ROWS, WIDTH), sds(FEAT, WIDTH)),
            in_specs=[smem, smem] + [hbm] * 5,
            out_specs=(hbm,) * 5,
            scratch_shapes=[
                buf(3, ROWS, WIDTH), buf(DEST, OUT), buf(NDP, FEAT, WIDTH), buf(ROWS, WIDTH), buf(4, SLOT, WIDTH),
                buf(4, SLOT, WIDTH), buf(DEST, WIDTH), buf(ROWS, WIDTH), buf(8, 2, SUB, WIDTH),
                buf(2, 4, 2, SUB, WIDTH), buf(2, SUB, WIDTH), buf(8, 2, SUB, WIDTH), buf(2, 4, 4, FEAT, WIDTH),
                buf(4, 4, FEAT, WIDTH), buf(3, 4, FEAT, WIDTH), buf(3, FEAT, WIDTH), buf(3, ROWS, WIDTH),
                buf(FEAT, WIDTH), pltpu.VMEM((DEST, WIDTH), F32),
                DMA((5,)), DMA((4,)), DMA((16,)), DMA((31,)), DMA((NDP,)), DMA((4,)), DMA((4,)),
                DMA((2, 4, 2)), DMA((2, 4, 2)), DMA((2,)), DMA((2,)), DMA((2, 4, 2)), DMA((2, 4, 2)),
                DMA((7,)), DMA((7,)),
            ],
            compiler_params=pltpu.CompilerParams(
                collective_id=turn, has_side_effects=True, vmem_limit_bytes=48 << 20
            ),
            name="layer_turn_%d" % turn,
        )

    first = -destinations[0, 0] & (NDP - 1)
    index = jnp.minimum(first, NDP - 1 - first)
    *outs, grad_weight = lax.switch(
        index,
        [branch(turn) for turn in range(NDP // 2)],
        patch_counts.T, destinations.T, queries, key_rows, value_rows, cotangent, out_weight.T,
    )
    return (*outs, grad_weight.T)


def solution(mesh):
    in_specs = (P("dp", "mp"), P("dp", "mp"), P("dp", "mp"), P("dp", None), P("mp", "dp"), P(), P())
    out_specs = (P("dp", None), P("dp", "mp"), P("dp", "mp"), P("dp", "mp"), P("mp", "dp"))
    return jax.shard_map(local, mesh=mesh, in_specs=in_specs, out_specs=out_specs, check_vma=False)
```

```python
import functools
import math

import jax
import jax.numpy as jnp
from jax import lax
from jax.experimental import pallas as pl
from jax.experimental.pallas import tpu as pltpu
from jax.sharding import PartitionSpec as P

HD = 128
HEADS = 3
NDP = 32
SLOT = 160
ROWS = 320
DEST = 256
FEAT = 96
WIDTH = HEADS * HD
OUT = 3072
SUB = DEST // 2
SCALE = 1.0 / math.sqrt(HD)
MESH = pl.DeviceIdType.MESH
F32 = jnp.float32
BF16 = jnp.bfloat16


def dot(a, b, dims):
    return lax.dot_general(a, b, (dims, ((), ())), preferred_element_type=F32)


def place():
    dp = lax.axis_index("dp")
    mp = lax.axis_index("mp")
    return dp, mp, dp // 8, (dp // 2) % 4, dp % 2, mp // 2, mp % 2


def block(i, size):
    return pl.ds(pl.multiple_of(i * size, size), size)


def dp_of(zh, x, core):
    return (zh * 4 + x) * 2 + core


def mod(a, n):
    return lax.rem(a + n, n)


def remote(src, dst, ss, rs, dp, mp):
    return pltpu.make_async_remote_copy(
        src_ref=src, dst_ref=dst, send_sem=ss, recv_sem=rs, device_id=(dp, mp), device_id_type=MESH
    )


def greet(peers):
    barrier = pltpu.get_barrier_semaphore()
    for dp, mp in peers:
        pl.semaphore_signal(barrier, inc=1, device_id=(dp, mp), device_id_type=MESH)


def greeted(count):
    pl.semaphore_wait(pltpu.get_barrier_semaphore(), count)


def tables(counts_ref, dests_ref, dp):
    first = mod(-dests_ref[0, 0], NDP)
    turn = jnp.minimum(first, NDP - 1 - first)
    swap = (first >= NDP // 2).astype(jnp.int32)
    c0 = counts_ref[0, dp]
    c1 = counts_ref[1, dp]
    home = (
        (jnp.where(swap == 1, c0, 0), jnp.where(swap == 1, c1, c0)),
        (jnp.where(swap == 1, 0, c0), jnp.where(swap == 1, c0, c1)),
    )
    src_a = lax.rem(dp + turn, NDP)
    src_b = mod(dp - turn - 1, NDP)
    count_a = counts_ref[swap, src_a]
    count_b = counts_ref[1 - swap, src_b]
    a_first = src_a < src_b
    dest = (
        (jnp.where(a_first, 0, count_b), count_a),
        (jnp.where(a_first, count_a, 0), count_b),
    )
    return home, dest, turn


def iota(shape, dim):
    return lax.broadcasted_iota(jnp.int32, shape, dim)


def pick(rows, start, count):
    shape = (SLOT, rows)
    r, c = iota(shape, 0), iota(shape, 1)
    return jnp.where((c == r + start) & (r < count), 1.0, 0.0).astype(BF16)


def put(rows, start, count):
    shape = (rows, SLOT)
    r, c = iota(shape, 0), iota(shape, 1)
    return jnp.where((r == c + start) & (c < count), 1.0, 0.0).astype(BF16)


def either(slot, pair):
    return [jnp.where(slot == 0, a, b) for a, b in zip(*pair)]


def probabilities(q, k, count):
    scores = dot(q, k, ((1,), (1,))) * SCALE
    scores = jnp.where(iota(scores.shape, 1) < count, scores, -1e30)
    weights = jnp.exp(scores - jnp.max(scores, axis=-1, keepdims=True))
    return weights / jnp.sum(weights, axis=-1, keepdims=True)


def load_rows(refs, qkv_ref, load, first):
    copies = [pltpu.make_async_copy(ref, qkv_ref.at[i], load.at[first + i]) for i, ref in enumerate(refs)]
    for copy in copies:
        copy.start()
    return copies


def pick_rows(rows_ref, qkv_ref, home):
    @pl.loop(0, 6)
    def _(i):
        picked = pick(ROWS, *either(i % 2, home))
        rows_ref[i // 2, i % 2] = dot(picked, qkv_ref[i // 2], ((1,), (0,))).astype(BF16)


def forward_kernel(counts_ref, dests_ref, q_hbm, k_hbm, v_hbm, out_ref, qkv_ref, rows_ref, load):
    home, _, _ = tables(counts_ref, dests_ref, lax.axis_index("dp"))
    for copy in load_rows((q_hbm, k_hbm, v_hbm), qkv_ref, load, 0):
        copy.wait()
    pick_rows(rows_ref, qkv_ref, home)

    @pl.loop(0, 6)
    def _(i):
        slot, cols = i % 2, block(i // 2, HD)
        probs = probabilities(rows_ref[0, slot, :, cols], rows_ref[1, slot, :, cols], either(slot, home)[1])
        out_ref[slot, :, cols] = dot(probs.astype(BF16), rows_ref[2, slot, :, cols], ((1,), (0,))).astype(BF16)


def turn_kernel(turn, in_ref, out_ref, ss, rs):
    dp, mp, *_ = place()
    routes = [(0, mod(dp - turn, NDP)), (1, lax.rem(dp + turn + 1, NDP))]
    others, own = (routes[1:], routes[:1]) if turn == 0 else (routes, [])
    greet([(p, mp) for _, p in others] + [(mod(2 * dp - p, NDP), mp) for _, p in others])
    local = [pltpu.make_async_copy(in_ref.at[i], out_ref.at[i], ss.at[i]) for i, _ in own]
    for copy in local:
        copy.start()
    greeted(2 * len(others))
    copies = [remote(in_ref.at[i], out_ref.at[i], ss.at[i], rs.at[i], p, mp) for i, p in others]
    for copy in copies:
        copy.start()
    for copy in local + copies:
        copy.wait()


def main_kernel(
    counts_ref, dests_ref, turned_ref, q_hbm, k_hbm, v_hbm, cot_hbm, w_hbm,
    att_hbm, gq_hbm, gk_hbm, gv_hbm, gw_hbm,
    qkv_ref, cot_ref, wt_ref, rows_ref, moved_ref, came_ref, dest_ref, part_ref, yring_ref, zring_ref, across_ref,
    half_ref, fold_ref, att_ref, term_ref, core_ref, xin_ref, zin_ref, grads_ref, gw_ref, sum_ref,
    load, store, att_store, wt_s, wt_r, turn_s, turn_r, ring_s, ring_r, fold_s, fold_r, gath_s, gath_r, pass_s, pass_r,
    red_s, red_r,
):
    dp, mp, zh, x, core, y, zl = place()
    up, down = lax.rem(y + 1, 8) * 2 + zl, lax.rem(y + 7, 8) * 2 + zl
    across = y * 2 + 1 - zl
    sibling = dp_of(zh, x, 1 - core)
    xs = [dp_of(zh, lax.rem(x + i, 4), core) for i in (1, 3, 2)]
    zs = [dp_of(lax.rem(zh + i, 4), x, core) for i in (1, 3, 2)]
    peers = [(dp, up), (dp, down), (dp, across)] + [(p, mp) for p in [sibling] + xs + zs]
    peers += [(lax.rem(dp + i, NDP), mp) for i in (1, 2, 4, 8, 24, 28, 30, 31)]
    greet(peers)

    loads = [pltpu.make_async_copy(w_hbm, wt_ref.at[dp], load.at[0]), pltpu.make_async_copy(cot_hbm, cot_ref, load.at[1])]
    for copy in loads:
        copy.start()
    loads += load_rows((q_hbm, k_hbm, v_hbm), qkv_ref, load, 2)
    home, dest, turn = tables(counts_ref, dests_ref, dp)
    pending = []

    def shard_send(i, shard, to):
        remote(wt_ref.at[shard], wt_ref.at[shard], wt_s.at[i], wt_r.at[shard], to, mp).start()

    def shard_wait(shard):
        remote(wt_ref.at[shard], wt_ref.at[shard], wt_s.at[0], wt_r.at[shard], dp, mp).wait_recv()

    def shard_sent(i):
        remote(wt_ref.at[dp], wt_ref.at[dp], wt_s.at[i], wt_r.at[dp], sibling, mp).wait_send()

    odd = lax.rem(y, 2)
    order = [lax.rem((y + 4) // 2 + i, 4) for i in (0, 3 - 2 * odd, 1 + 2 * odd, 2)]

    def z_arrive(i):
        @pl.when(order[i] != zh)
        def _():
            shard = dp_of(order[i], x, core)
            shard_wait(shard)
            for j, p in enumerate(xs + [sibling]):
                shard_send(7 + 4 * i + j, shard, p)

    def x_arrive(i):
        for j in range(3):
            shard = dp_of(order[i], lax.rem(x + (1, 3, 2)[j], 4), core)
            shard_wait(shard)
            shard_send(23 + 3 * i + j, shard, sibling)
        for j in range(4):
            shard_wait(dp_of(order[i], j, 1 - core))

    def partial(i):
        for j in range(2):
            c = 2 * order[i] + j
            w = wt_ref[pl.ds(4 * c, 4)].reshape(WIDTH, WIDTH)
            part_ref[lax.rem(c - y + 8, 8)] = dot(dest_ref[...], w, ((1,), (1,))).astype(BF16)

    loads[0].wait()
    greeted(len(peers))
    for i, p in enumerate(zs + xs + [sibling]):
        shard_send(i, dp, p)

    def place_rows(ref, parts, spans):
        @pl.loop(0, ref.shape[0] // 64)
        def _(i):
            rows = 0.0
            for part, (start, count) in zip(parts, spans):
                rows = rows + dot(put(64, start - 64 * i, count), part[...], ((1,), (0,)))
            ref[block(i, 64)] = rows.astype(BF16)

    place_rows(dest_ref, [turned_ref.at[0], turned_ref.at[1]], dest)
    loads[1].wait()

    @pl.loop(0, 8)
    def _(c):
        term = dot(cot_ref[:, block(c, WIDTH)], dest_ref[...], ((0,), (0,))).astype(BF16)
        for i in range(4):
            term_ref[i % 2, lax.rem(2 * c + i // 2, 4), c // 2] = term[i * FEAT : (i + 1) * FEAT]

    for i in range(4):
        z_arrive(i)
    swap = remote(term_ref.at[1 - core], core_ref, red_s.at[0], red_r.at[0], sibling, mp)
    swap.start()
    pending.append(swap)
    for i in range(2):
        x_arrive(i)

    mine, other = pl.ds(pl.multiple_of(64 * zl, 64), 64), pl.ds(pl.multiple_of(64 - 64 * zl, 64), 64)
    low_mine = pl.ds(pl.multiple_of(SUB + 64 * zl, 64), 64)
    low_other = pl.ds(pl.multiple_of(SUB + 64 - 64 * zl, 64), 64)

    def ring_copy(zone, way, step):
        c = 4 - step if way == 0 else 4 + step
        src = half_ref.at[c] if zone else part_ref.at[c, pl.ds(0, SUB)]
        dst = (zring_ref if zone else yring_ref).at[way, step]
        sem = (zone, way, step)
        return remote(src, dst, ring_s.at[sem], ring_r.at[sem], dp, up if way == 0 else down)

    def ring_send(zone, way, step):
        ring_copy(zone, way, step).start()

    def ring_take(zone, way, step):
        ring_copy(zone, way, step).wait_recv()
        c = 3 - step if way == 0 else 5 + step
        ref = half_ref.at[c] if zone else part_ref.at[c, pl.ds(0, SUB)]
        add(ref, ref, (zring_ref if zone else yring_ref).at[way, step])

    def add(out, *refs):
        @pl.loop(0, out.shape[0] // 32)
        def _(i):
            total = 0.0
            for ref in refs:
                total = total + ref[block(i, 32)].astype(F32)
            out[block(i, 32)] = total.astype(BF16)

    shares = []

    def share_send(lo, hi):
        i, span = len(shares), pl.ds(lo, hi - lo)
        copy = remote(part_ref.at[span, low_other], across_ref.at[span], fold_s.at[i], fold_r.at[i], dp, across)
        copy.start()
        shares.append((copy, lo, hi))
        pending.append(copy)

    def share_take(i):
        copy, lo, hi = shares[i]
        copy.wait_recv()

        @pl.loop(lo, hi)
        def _(c):
            add(half_ref.at[c], part_ref.at[c, low_mine], across_ref.at[c])

    partial(0)
    partial(1)
    ring_send(0, 0, 0)
    ring_send(0, 1, 1)
    share_send(3, 6)
    x_arrive(2)
    partial(2)
    share_take(0)
    ring_send(1, 1, 0)
    ring_send(1, 0, 1)
    x_arrive(3)
    partial(3)
    share_send(0, 3)
    share_send(6, 8)
    ring_take(0, 0, 0)
    ring_send(0, 0, 1)

    sum_ref[...] = jnp.zeros_like(sum_ref)

    @pl.loop(0, 8)
    def _(c):
        w = wt_ref[pl.ds(4 * c, 4)].reshape(WIDTH, WIDTH)
        sum_ref[...] += dot(cot_ref[:, block(c, WIDTH)], w, ((1,), (0,)))

    moved_ref[1, 0] = dot(pick(DEST, *dest[0]), sum_ref[...].astype(BF16), ((1,), (0,))).astype(BF16)
    moved_ref[0, 1] = dot(pick(DEST, *dest[1]), sum_ref[...].astype(BF16), ((1,), (0,))).astype(BF16)

    def shift_copy(i, slot):
        by = (1, 8, 4, 2, 1)[i]
        to = mod(dp - by, NDP) if slot else lax.rem(dp + by, NDP)
        dst = came_ref.at[i, slot] if i else moved_ref.at[1, 1]
        return remote(moved_ref.at[i, slot], dst, turn_s.at[i, slot], turn_r.at[i, slot], to, mp)

    def shift_send(i):
        for slot in range(0 if i else 1, 2):
            shift_copy(i, slot).start()
            pending.append(shift_copy(i, slot))

    def shift_take(i):
        for slot in range(0 if i else 1, 2):
            shift_copy(i, slot).wait_recv()
            if i:
                taken = lax.rem(turn // (1, 8, 4, 2, 1)[i], 2) == 1
                moved_ref[i + 1, slot] = jnp.where(taken, came_ref[i, slot], moved_ref[i, slot])

    shift_send(0)

    swap.wait_recv()
    @pl.loop(0, 16)
    def _(i):
        ref = term_ref.at[core, i // 4, lax.rem(i, 4)]
        add(ref, ref, core_ref.at[i // 4, lax.rem(i, 4)])

    xcopies = []
    for n, i in enumerate((1, 3, 2)):
        copy = remote(term_ref.at[core, lax.rem(x + i, 4)], xin_ref.at[n], red_s.at[1 + n], red_r.at[1 + n], xs[n], mp)
        copy.start()
        xcopies.append(copy)
    pending.extend(xcopies)

    share_take(1)
    share_take(2)
    ring_take(1, 1, 0)
    ring_send(1, 1, 1)
    shift_take(0)
    shift_send(1)
    for step in (1, 2):
        for zone, way in ((0, 1), (1, 0), (0, 0), (1, 1)):
            ring_take(zone, way, step)
            ring_send(zone, way, step + 1)
    shift_take(1)
    shift_send(2)
    loads[2].wait()
    loads[3].wait()
    loads[4].wait()
    pick_rows(rows_ref, qkv_ref, home)

    for way in range(2):
        ring_copy(0, way, 3).wait_recv()
    own = part_ref.at[0, pl.ds(0, SUB)]
    add(own, own, yring_ref.at[0, 3], yring_ref.at[1, 3])
    fold = remote(part_ref.at[0, other], fold_ref, fold_s.at[3], fold_r.at[3], dp, across)
    fold.start()
    for way in range(2):
        ring_copy(1, way, 3).wait_recv()
    add(att_ref.at[0, low_mine], half_ref.at[0], zring_ref.at[0, 3], zring_ref.at[1, 3])

    def low_copy(rows):
        return remote(att_ref.at[0, rows], att_ref.at[0, rows], fold_s.at[4], fold_r.at[4], dp, across)

    low_copy(low_mine).start()
    pending.extend([fold, low_copy(low_mine)])

    def att_copy(zone, c):
        rows, cols = pl.ds(zone * SUB, SUB), block(lax.rem(y + c, 8), WIDTH)
        return pltpu.make_async_copy(att_ref.at[c, rows], att_hbm.at[rows, cols], att_store.at[zone, c])

    def gather_copy(zone, way, step):
        rows = pl.ds(SUB, SUB) if zone else mine
        src, dst = (lax.rem(8 - step, 8), 7 - step) if way == 0 else (step, step + 1)
        sem = (zone, way, step)
        return remote(
            att_ref.at[src, rows], att_ref.at[dst, rows], gath_s.at[sem], gath_r.at[sem], dp, up if way == 0 else down
        )

    def gather_send(zone, way, step):
        gather_copy(zone, way, step).start()

    def pass_copy(c, rows):
        return remote(att_ref.at[c, rows], att_ref.at[c, rows], pass_s.at[c], pass_r.at[c], dp, across)

    def gather_take(zone, way, step):
        gather_copy(zone, way, step).wait_recv()
        c = 7 - step if way == 0 else step + 1
        if zone:
            att_copy(1, c).start()
        else:
            pass_copy(c, mine).start()

    fold.wait_recv()
    add(att_ref.at[0, mine], part_ref.at[0, mine], fold_ref)
    gather_send(0, 0, 0)
    gather_send(0, 1, 0)
    pass_copy(0, mine).start()
    low_copy(low_other).wait_recv()
    gather_send(1, 0, 0)
    gather_send(1, 1, 0)
    att_copy(1, 0).start()

    for copy in xcopies:
        copy.wait_recv()

    @pl.loop(0, 4)
    def _(i):
        add(term_ref.at[core, x, i], term_ref.at[core, x, i], *[xin_ref.at[n, i] for n in range(3)])

    zcopies = []
    for n, i in enumerate((1, 3, 2)):
        copy = remote(
            term_ref.at[core, x, lax.rem(zh + i, 4)], zin_ref.at[n], red_s.at[4 + n], red_r.at[4 + n], zs[n], mp
        )
        copy.start()
        zcopies.append(copy)
    pending.extend(zcopies)

    outs = []
    shift_take(2)
    shift_send(3)
    for step in range(2):
        for zone, way in ((0, 0), (0, 1), (1, 0), (1, 1)):
            gather_take(zone, way, step)
            gather_send(zone, way, step + 1)
        shift_take(3 + step)
        if step == 0:
            shift_send(4)

    @pl.loop(0, 6)
    def _(i):
        slot, cols = i % 2, block(i // 2, HD)
        q, k, v = rows_ref[0, slot, :, cols], rows_ref[1, slot, :, cols], rows_ref[2, slot, :, cols]
        gm = moved_ref[5, slot, :, cols]
        probs = probabilities(q, k, either(slot, home)[1])
        gp = dot(gm, v, ((1,), (1,)))
        inner = jnp.sum(gp * probs, axis=-1, keepdims=True)
        gs = (probs * (gp - inner) * SCALE).astype(BF16)
        rows_ref[0, slot, :, cols] = dot(gs, k, ((1,), (0,))).astype(BF16)
        rows_ref[1, slot, :, cols] = dot(gs, q, ((0,), (0,))).astype(BF16)
        rows_ref[2, slot, :, cols] = dot(probs.astype(BF16), gm, ((0,), (0,))).astype(BF16)

    @pl.loop(0, 3)
    def _(i):
        place_rows(grads_ref.at[i], [rows_ref.at[i, 0], rows_ref.at[i, 1]], home)

    for i, ref in enumerate((gq_hbm, gk_hbm, gv_hbm)):
        outs.append(pltpu.make_async_copy(grads_ref.at[i], ref, store.at[i]))
    for copy in outs:
        copy.start()

    for zone, way in ((0, 1), (1, 0), (0, 0), (1, 1)):
        gather_take(zone, way, 2)
        if zone != way:
            gather_send(zone, way, 3)
    for copy in zcopies:
        copy.wait_recv()
    add(gw_ref, term_ref.at[core, x, zh], *[zin_ref.at[n] for n in range(3)])
    outs.append(pltpu.make_async_copy(gw_ref, gw_hbm, store.at[3]))
    outs[-1].start()
    gather_take(0, 1, 3)
    gather_take(1, 0, 3)

    @pl.loop(0, 8)
    def _(c):
        pass_copy(c, other).wait_recv()
        att_copy(0, c).start()

    for copy in outs:
        copy.wait()

    @pl.loop(0, 8)
    def _(c):
        att_copy(0, c).wait()
        att_copy(1, c).wait()
        pass_copy(c, mine).wait_send()

    for zone in range(2):
        for way in range(2):
            @pl.loop(0 if zone == way else 1, 4)
            def _(step):
                ring_copy(zone, way, step).wait_send()

            @pl.loop(0, 3 if zone == way else 4)
            def _(step):
                gather_copy(zone, way, step).wait_send()

    for i in range(4):

        @pl.when(order[i] != zh)
        def _():
            for j in range(4):
                shard_sent(7 + 4 * i + j)

    for i in [*range(7), *range(23, 35)]:
        shard_sent(i)
    for copy in pending:
        copy.wait_send()


def sds(*shape):
    return jax.ShapeDtypeStruct(shape, BF16)


def buf(*shape):
    return pltpu.VMEM(shape, BF16)


DMA = pltpu.SemaphoreType.DMA


def local(queries, key_rows, value_rows, cotangent, out_weight, patch_counts, destinations):
    smem, hbm, vmem = [pl.BlockSpec(memory_space=space) for space in (pltpu.SMEM, pl.ANY, pltpu.VMEM)]
    counts, dests = patch_counts.T, destinations.T
    mixed = pl.pallas_call(
        forward_kernel,
        out_shape=sds(2, SLOT, WIDTH),
        in_specs=[smem, smem] + [hbm] * 3,
        out_specs=vmem,
        scratch_shapes=[buf(3, ROWS, WIDTH), buf(3, 2, SLOT, WIDTH), DMA((3,))],
        compiler_params=pltpu.CompilerParams(vmem_limit_bytes=32 << 20),
        name="forward",
    )(counts, dests, queries, key_rows, value_rows)

    def branch(turn):
        return pl.pallas_call(
            functools.partial(turn_kernel, turn),
            out_shape=sds(2, SLOT, WIDTH),
            in_specs=[vmem],
            out_specs=vmem,
            scratch_shapes=[DMA((2,)), DMA((2,))],
            compiler_params=pltpu.CompilerParams(collective_id=1 + turn, has_side_effects=True),
            name="turn_%d" % turn,
        )

    first = -destinations[0, 0] & (NDP - 1)
    index = jnp.minimum(first, NDP - 1 - first)
    turned = lax.switch(index, [branch(turn) for turn in range(NDP // 2)], mixed)

    *outs, grad_weight = pl.pallas_call(
        main_kernel,
        out_shape=(sds(DEST, OUT), sds(ROWS, WIDTH), sds(ROWS, WIDTH), sds(ROWS, WIDTH), sds(FEAT, WIDTH)),
        in_specs=[smem, smem, vmem] + [hbm] * 5,
        out_specs=(hbm,) * 5,
        scratch_shapes=[
            buf(3, ROWS, WIDTH), buf(DEST, OUT), buf(NDP, FEAT, WIDTH), buf(3, 2, SLOT, WIDTH),
            buf(6, 2, SLOT, WIDTH), buf(5, 2, SLOT, WIDTH), buf(DEST, WIDTH), buf(8, DEST, WIDTH),
            buf(2, 4, SUB, WIDTH), buf(2, 4, 64, WIDTH), buf(8, 64, WIDTH), buf(8, 64, WIDTH), buf(64, WIDTH),
            buf(8, DEST, WIDTH), buf(2, 4, 4, FEAT, WIDTH), buf(4, 4, FEAT, WIDTH), buf(3, 4, FEAT, WIDTH),
            buf(3, FEAT, WIDTH), buf(3, ROWS, WIDTH), buf(FEAT, WIDTH), pltpu.VMEM((DEST, WIDTH), F32),
            DMA((5,)), DMA((4,)), DMA((2, 8)), DMA((35,)), DMA((NDP,)), DMA((5, 2)), DMA((5, 2)),
            DMA((2, 2, 4)), DMA((2, 2, 4)), DMA((5,)), DMA((5,)), DMA((2, 2, 4)), DMA((2, 2, 4)),
            DMA((8,)), DMA((8,)), DMA((7,)), DMA((7,)),
        ],
        compiler_params=pltpu.CompilerParams(collective_id=0, has_side_effects=True, vmem_limit_bytes=40 << 20),
        name="project_backward",
    )(counts, dests, turned, queries, key_rows, value_rows, cotangent, out_weight.T)
    return (*outs, grad_weight.T)


def solution(mesh):
    in_specs = (P("dp", "mp"), P("dp", "mp"), P("dp", "mp"), P("dp", None), P("mp", "dp"), P(), P())
    out_specs = (P("dp", None), P("dp", "mp"), P("dp", "mp"), P("dp", "mp"), P("mp", "dp"))
    return jax.shard_map(local, mesh=mesh, in_specs=in_specs, out_specs=out_specs, check_vma=False)
```

```python
import functools
import math

import jax
import jax.numpy as jnp
from jax import lax
from jax.experimental import pallas as pl
from jax.experimental.pallas import tpu as pltpu
from jax.sharding import PartitionSpec as P

HD = 128
HEADS = 3
NDP = 32
SLOT = 160
ROWS = 320
DEST = 256
FEAT = 96
WIDTH = HEADS * HD
OUT = 3072
SUB = DEST // 2
SCALE = 1.0 / math.sqrt(HD)
MESH = pl.DeviceIdType.MESH
F32 = jnp.float32
BF16 = jnp.bfloat16


def dot(a, b, dims):
    return lax.dot_general(a, b, (dims, ((), ())), preferred_element_type=F32)


def place():
    dp = lax.axis_index("dp")
    mp = lax.axis_index("mp")
    return dp, mp, dp // 8, (dp // 2) % 4, dp % 2, mp // 2, mp % 2


def block(i, size):
    return pl.ds(pl.multiple_of(i * size, size), size)


def dp_of(zh, x, core):
    return (zh * 4 + x) * 2 + core


def mod(a, n):
    return lax.rem(a + n, n)


def remote(src, dst, ss, rs, dp, mp):
    return pltpu.make_async_remote_copy(
        src_ref=src, dst_ref=dst, send_sem=ss, recv_sem=rs, device_id=(dp, mp), device_id_type=MESH
    )


def greet(peers):
    barrier = pltpu.get_barrier_semaphore()
    for dp, mp in peers:
        pl.semaphore_signal(barrier, inc=1, device_id=(dp, mp), device_id_type=MESH)


def greeted(count):
    pl.semaphore_wait(pltpu.get_barrier_semaphore(), count)


def tables(counts_ref, dests_ref, dp):
    first = mod(-dests_ref[0, 0], NDP)
    turn = jnp.minimum(first, NDP - 1 - first)
    swap = (first >= NDP // 2).astype(jnp.int32)
    c0 = counts_ref[0, dp]
    c1 = counts_ref[1, dp]
    home = (
        (jnp.where(swap == 1, c0, 0), jnp.where(swap == 1, c1, c0)),
        (jnp.where(swap == 1, 0, c0), jnp.where(swap == 1, c0, c1)),
    )
    src_a = lax.rem(dp + turn, NDP)
    src_b = mod(dp - turn - 1, NDP)
    count_a = counts_ref[swap, src_a]
    count_b = counts_ref[1 - swap, src_b]
    a_first = src_a < src_b
    dest = (
        (jnp.where(a_first, 0, count_b), count_a),
        (jnp.where(a_first, count_a, 0), count_b),
    )
    return home, dest, turn


def iota(shape, dim):
    return lax.broadcasted_iota(jnp.int32, shape, dim)


def pick(rows, start, count):
    shape = (SLOT, rows)
    r, c = iota(shape, 0), iota(shape, 1)
    return jnp.where((c == r + start) & (r < count), 1.0, 0.0).astype(BF16)


def put(rows, start, count):
    shape = (rows, SLOT)
    r, c = iota(shape, 0), iota(shape, 1)
    return jnp.where((r == c + start) & (c < count), 1.0, 0.0).astype(BF16)


def either(slot, pair):
    return [jnp.where(slot == 0, a, b) for a, b in zip(*pair)]


def probabilities(q, k, count):
    scores = dot(q, k, ((1,), (1,))) * SCALE
    scores = jnp.where(iota(scores.shape, 1) < count, scores, -1e30)
    weights = jnp.exp(scores - jnp.max(scores, axis=-1, keepdims=True))
    return weights / jnp.sum(weights, axis=-1, keepdims=True)


def load_rows(refs, qkv_ref, load, first):
    copies = [pltpu.make_async_copy(ref, qkv_ref.at[i], load.at[first + i]) for i, ref in enumerate(refs)]
    for copy in copies:
        copy.start()
    return copies


def pick_rows(rows_ref, qkv_ref, home):
    @pl.loop(0, 6)
    def _(i):
        picked = pick(ROWS, *either(i % 2, home))
        rows_ref[i // 2, i % 2] = dot(picked, qkv_ref[i // 2], ((1,), (0,))).astype(BF16)


def add(out, *refs):
    @pl.loop(0, out.shape[0] // 32)
    def _(i):
        total = 0.0
        for ref in refs:
            total = total + ref[block(i, 32)].astype(F32)
        out[block(i, 32)] = total.astype(BF16)


def place_rows(ref, parts, spans):
    @pl.loop(0, ref.shape[0] // 64)
    def _(i):
        rows = 0.0
        for part, (start, count) in zip(parts, spans):
            rows = rows + dot(put(64, start - 64 * i, count), part[...], ((1,), (0,)))
        ref[block(i, 64)] = rows.astype(BF16)


def gather_kernel(
    counts_ref, dests_ref, q_hbm, k_hbm, v_hbm, cot_hbm, w_hbm, slots_ref, wt_hbm,
    qkv_ref, cot_ref, wt_ref, rows_ref, sum_ref, load, store, wt_s, wt_r,
):
    dp, mp, zh, x, core, *_ = place()
    sibling = dp_of(zh, x, 1 - core)
    xs = [dp_of(zh, lax.rem(x + i, 4), core) for i in (1, 3, 2)]
    zs = [dp_of(lax.rem(zh + i, 4), x, core) for i in (1, 3, 2)]
    greet([(p, mp) for p in [sibling] + xs + zs])
    loads = [pltpu.make_async_copy(w_hbm, wt_ref.at[dp], load.at[0]), pltpu.make_async_copy(cot_hbm, cot_ref, load.at[1])]
    loads[0].start()
    loads += load_rows((q_hbm, k_hbm, v_hbm), qkv_ref, load, 2)
    loads[1].start()
    home, dest, _ = tables(counts_ref, dests_ref, dp)

    def shard_copy(i, shard, to):
        return remote(wt_ref.at[shard], wt_ref.at[shard], wt_s.at[i], wt_r.at[shard], to, mp)

    loads[0].wait()
    greeted(7)
    for i, p in enumerate(zs + xs + [sibling]):
        shard_copy(i, dp, p).start()

    for copy in loads[2:]:
        copy.wait()
    pick_rows(rows_ref, qkv_ref, home)

    @pl.loop(0, 6)
    def _(i):
        slot, cols = i % 2, block(i // 2, HD)
        probs = probabilities(rows_ref[0, slot, :, cols], rows_ref[1, slot, :, cols], either(slot, home)[1])
        slots_ref[slot, :, cols] = dot(probs.astype(BF16), rows_ref[2, slot, :, cols], ((1,), (0,))).astype(BF16)

    for i in range(3):
        shard_copy(0, zs[i], dp).wait_recv()
        for j, p in enumerate(xs + [sibling]):
            shard_copy(7 + 4 * i + j, zs[i], p).start()
    for i in range(4):
        for j in range(3):
            shard = dp_of(lax.rem(zh + (0, 1, 3, 2)[i], 4), lax.rem(x + (1, 3, 2)[j], 4), core)
            shard_copy(0, shard, dp).wait_recv()
            shard_copy(19 + 3 * i + j, shard, sibling).start()

    @pl.loop(0, 16)
    def _(i):
        shard_copy(0, 2 * i + 1 - core, dp).wait_recv()

    store_wt = pltpu.make_async_copy(wt_ref, wt_hbm, store.at[0])
    store_wt.start()
    loads[1].wait()
    sum_ref[...] = jnp.zeros_like(sum_ref)

    @pl.loop(0, 8)
    def _(c):
        w = wt_ref[pl.ds(4 * c, 4)].reshape(WIDTH, WIDTH)
        sum_ref[...] += dot(cot_ref[:, block(c, WIDTH)], w, ((1,), (0,)))

    for slot in range(2):
        slots_ref[2 + slot] = dot(pick(DEST, *dest[slot]), sum_ref[...].astype(BF16), ((1,), (0,))).astype(BF16)

    @pl.loop(0, 31)
    def _(i):
        shard_copy(i, dp, sibling).wait_send()

    store_wt.wait()


def turn_kernel(turn, in_ref, out_ref, ss, rs):
    dp, mp, *_ = place()
    back_a, on_a = mod(dp - turn, NDP), lax.rem(dp + turn, NDP)
    on_b, back_b = lax.rem(dp + turn + 1, NDP), mod(dp - turn - 1, NDP)
    routes = [(0, back_a), (1, on_b), (2, on_a), (3, back_b)]
    others, own = (routes[1::2], routes[::2]) if turn == 0 else (routes, [])
    greet([(p, mp) for _, p in others])
    local = [pltpu.make_async_copy(in_ref.at[i], out_ref.at[i], ss.at[i]) for i, _ in own]
    for copy in local:
        copy.start()
    greeted(len(others))
    copies = [remote(in_ref.at[i], out_ref.at[i], ss.at[i], rs.at[i], p, mp) for i, p in others]
    for copy in copies:
        copy.start()
    for copy in local + copies:
        copy.wait()


def main_kernel(
    counts_ref, dests_ref, turned_ref, q_hbm, k_hbm, v_hbm, cot_hbm, wt_hbm,
    att_hbm, gq_hbm, gk_hbm, gv_hbm, gw_hbm,
    qkv_ref, cot_ref, wt_ref, rows_ref, dest_ref, part_ref, ring_ref, across_ref, half_ref, fold_ref, att_ref,
    term_ref, core_ref, xin_ref, zin_ref, grads_ref, gw_ref,
    load, store, att_store, ring_s, ring_r, fold_s, fold_r, gath_s, gath_r, pass_s, pass_r, red_s, red_r,
):
    dp, mp, zh, x, core, y, zl = place()
    up, down = lax.rem(y + 1, 8) * 2 + zl, lax.rem(y + 7, 8) * 2 + zl
    across = y * 2 + 1 - zl
    sibling = dp_of(zh, x, 1 - core)
    xs = [dp_of(zh, lax.rem(x + i, 4), core) for i in (1, 3, 2)]
    zs = [dp_of(lax.rem(zh + i, 4), x, core) for i in (1, 3, 2)]
    greet([(dp, up), (dp, down), (dp, across)] + [(p, mp) for p in [sibling] + xs + zs])
    loads = [pltpu.make_async_copy(wt_hbm, wt_ref, load.at[0]), pltpu.make_async_copy(cot_hbm, cot_ref, load.at[1])]
    for copy in loads:
        copy.start()
    loads += load_rows((q_hbm, k_hbm, v_hbm), qkv_ref, load, 2)
    home, dest, _ = tables(counts_ref, dests_ref, dp)
    place_rows(dest_ref, [turned_ref.at[0], turned_ref.at[1]], dest)
    pending = []

    mine, other = pl.ds(pl.multiple_of(64 * zl, 64), 64), pl.ds(pl.multiple_of(64 - 64 * zl, 64), 64)
    low_mine = pl.ds(pl.multiple_of(SUB + 64 * zl, 64), 64)
    low_other = pl.ds(pl.multiple_of(SUB + 64 - 64 * zl, 64), 64)

    def ring_ref_of(zone, c):
        return half_ref.at[c] if zone == 2 else part_ref.at[c, pl.ds(64 * zone, 64)]

    def ring_copy(zone, way, step):
        c = 4 - step if way == 0 else 4 + step
        sem = (zone, way, step)
        return remote(ring_ref_of(zone, c), ring_ref.at[sem], ring_s.at[sem], ring_r.at[sem], dp, (up, down)[way])

    def ring_send(zone, way, step):
        copy = ring_copy(zone, way, step)
        copy.start()
        pending.append(copy)

    def ring_take(zone, way, step):
        ring_copy(zone, way, step).wait_recv()
        ref = ring_ref_of(zone, 3 - step if way == 0 else 5 + step)
        add(ref, ref, ring_ref.at[zone, way, step])

    def partial(c):
        w = wt_ref[pl.ds(4 * lax.rem(y + c, 8), 4)].reshape(WIDTH, WIDTH)
        part_ref[c] = dot(dest_ref[...], w, ((1,), (1,))).astype(BF16)

    shares = []

    def share_send(lo, hi):
        i, span = len(shares), pl.ds(lo, hi - lo)
        copy = remote(part_ref.at[span, low_other], across_ref.at[span], fold_s.at[i], fold_r.at[i], dp, across)
        copy.start()
        shares.append((copy, lo, hi))
        pending.append(copy)

    def share_take(i):
        copy, lo, hi = shares[i]
        copy.wait_recv()

        @pl.loop(lo, hi)
        def _(c):
            add(half_ref.at[c], part_ref.at[c, low_mine], across_ref.at[c])

    loads[0].wait()
    pl.loop(3, 6)(partial)
    greeted(10)
    for zone in range(2):
        ring_send(zone, 0, 0)
        ring_send(zone, 1, 1)
    share_send(3, 6)
    pl.loop(0, 3)(partial)
    share_send(0, 3)
    pl.loop(6, 8)(partial)
    share_send(6, 8)

    loads[1].wait()

    @pl.loop(0, 8)
    def _(c):
        term = dot(cot_ref[:, block(c, WIDTH)], dest_ref[...], ((0,), (0,))).astype(BF16)
        for i in range(4):
            term_ref[i % 2, lax.rem(2 * c + i // 2, 4), c // 2] = term[i * FEAT : (i + 1) * FEAT]

    swap = remote(term_ref.at[1 - core], core_ref, red_s.at[0], red_r.at[0], sibling, mp)
    swap.start()
    pending.append(swap)
    for zone in range(2):
        ring_take(zone, 0, 0)
        ring_send(zone, 0, 1)
    share_take(0)
    ring_send(2, 1, 0)
    ring_send(2, 0, 1)

    swap.wait_recv()

    @pl.loop(0, 16)
    def _(i):
        ref = term_ref.at[core, i // 4, lax.rem(i, 4)]
        add(ref, ref, core_ref.at[i // 4, lax.rem(i, 4)])

    xcopies = []
    for n, i in enumerate((1, 3, 2)):
        copy = remote(term_ref.at[core, lax.rem(x + i, 4)], xin_ref.at[n], red_s.at[1 + n], red_r.at[1 + n], xs[n], mp)
        copy.start()
        xcopies.append(copy)
    pending.extend(xcopies)
    share_take(1)
    share_take(2)

    def ring_step(zone, way, step):
        ring_take(zone, way, step)
        ring_send(zone, way, step + 1)

    for zone, way in ((0, 1), (1, 1), (0, 0), (1, 0)):
        ring_step(zone, way, 1)
    ring_step(2, 1, 0)
    ring_step(2, 0, 1)
    for zone, way in ((0, 1), (1, 1), (0, 0), (1, 0)):
        ring_step(zone, way, 2)
    ring_step(2, 1, 1)
    ring_step(2, 0, 2)
    ring_step(2, 1, 2)

    for zone in range(2):
        for way in range(2):
            ring_copy(zone, way, 3).wait_recv()
        own = ring_ref_of(zone, 0)
        add(own, own, ring_ref.at[zone, 0, 3], ring_ref.at[zone, 1, 3])
    fold = remote(part_ref.at[0, other], fold_ref, fold_s.at[3], fold_r.at[3], dp, across)
    fold.start()
    for way in range(2):
        ring_copy(2, way, 3).wait_recv()
    add(att_ref.at[0, low_mine], half_ref.at[0], ring_ref.at[2, 0, 3], ring_ref.at[2, 1, 3])

    def low_copy(rows):
        return remote(att_ref.at[0, rows], att_ref.at[0, rows], fold_s.at[4], fold_r.at[4], dp, across)

    low_copy(low_mine).start()
    pending.extend([fold, low_copy(low_mine)])

    def att_copy(part, c):
        rows, cols = pl.ds(part * SUB, SUB), block(lax.rem(y + c, 8), WIDTH)
        return pltpu.make_async_copy(att_ref.at[c, rows], att_hbm.at[rows, cols], att_store.at[part, c])

    def gather_copy(zone, way, step):
        rows = mine if zone == 2 else pl.ds(SUB + 64 * zone, 64)
        src, dst = ((8 - step) % 8, 7 - step) if way == 0 else (step, step + 1)
        sem = (zone, way, step)
        return remote(
            att_ref.at[src, rows], att_ref.at[dst, rows], gath_s.at[sem], gath_r.at[sem], dp, (up, down)[way]
        )

    def gather_send(zone, way, step):
        copy = gather_copy(zone, way, step)
        copy.start()
        pending.append(copy)

    def pass_copy(c, rows):
        return remote(att_ref.at[c, rows], att_ref.at[c, rows], pass_s.at[c], pass_r.at[c], dp, across)

    def gather_take(zone, way, step):
        gather_copy(zone, way, step).wait_recv()
        c = 7 - step if way == 0 else step + 1
        if zone == 2:
            pass_copy(c, mine).start()
        elif zone == 1:
            att_copy(1, c).start()

    fold.wait_recv()
    add(att_ref.at[0, mine], part_ref.at[0, mine], fold_ref)
    gather_send(2, 0, 0)
    gather_send(2, 1, 0)
    pass_copy(0, mine).start()
    low_copy(low_other).wait_recv()
    for zone in range(2):
        gather_send(zone, 0, 0)
        gather_send(zone, 1, 0)
    att_copy(1, 0).start()

    for copy in loads[2:]:
        copy.wait()
    pick_rows(rows_ref, qkv_ref, home)

    @pl.loop(0, 6)
    def _(i):
        slot, cols = i % 2, block(i // 2, HD)
        q, k, v = rows_ref[0, slot, :, cols], rows_ref[1, slot, :, cols], rows_ref[2, slot, :, cols]
        gm = turned_ref[2 + slot, :, cols]
        probs = probabilities(q, k, either(slot, home)[1])
        gp = dot(gm, v, ((1,), (1,)))
        inner = jnp.sum(gp * probs, axis=-1, keepdims=True)
        gs = (probs * (gp - inner) * SCALE).astype(BF16)
        rows_ref[0, slot, :, cols] = dot(gs, k, ((1,), (0,))).astype(BF16)
        rows_ref[1, slot, :, cols] = dot(gs, q, ((0,), (0,))).astype(BF16)
        rows_ref[2, slot, :, cols] = dot(probs.astype(BF16), gm, ((0,), (0,))).astype(BF16)

    outs = []
    for zone, way in ((2, 0), (2, 1), (0, 0), (0, 1), (1, 0), (1, 1)):
        gather_take(zone, way, 0)
        gather_send(zone, way, 1)
    for copy in xcopies:
        copy.wait_recv()

    @pl.loop(0, 4)
    def _(i):
        add(term_ref.at[core, x, i], term_ref.at[core, x, i], *[xin_ref.at[n, i] for n in range(3)])

    zcopies = []
    for n, i in enumerate((1, 3, 2)):
        copy = remote(
            term_ref.at[core, x, lax.rem(zh + i, 4)], zin_ref.at[n], red_s.at[4 + n], red_r.at[4 + n], zs[n], mp
        )
        copy.start()
        zcopies.append(copy)
    pending.extend(zcopies)

    @pl.loop(0, 3)
    def _(i):
        place_rows(grads_ref.at[i], [rows_ref.at[i, 0], rows_ref.at[i, 1]], home)

    for i, ref in enumerate((gq_hbm, gk_hbm, gv_hbm)):
        outs.append(pltpu.make_async_copy(grads_ref.at[i], ref, store.at[i]))
    for copy in outs:
        copy.start()
    for zone, way in ((2, 0), (2, 1), (0, 0), (0, 1), (1, 0), (1, 1)):
        gather_take(zone, way, 1)
        gather_send(zone, way, 2)
    for zone, way in ((2, 0), (2, 1), (0, 0), (0, 1), (1, 0), (1, 1)):
        gather_take(zone, way, 2)
        if way == zone // 2:
            gather_send(zone, way, 3)
    for copy in zcopies:
        copy.wait_recv()
    add(gw_ref, term_ref.at[core, x, zh], *[zin_ref.at[n] for n in range(3)])
    outs.append(pltpu.make_async_copy(gw_ref, gw_hbm, store.at[3]))
    outs[-1].start()
    for zone in (2, 0, 1):
        gather_take(zone, zone // 2, 3)

    @pl.loop(0, 8)
    def _(c):
        pass_copy(c, other).wait_recv()
        att_copy(0, c).start()

    for copy in outs:
        copy.wait()

    @pl.loop(0, 8)
    def _(c):
        att_copy(0, c).wait()
        att_copy(1, c).wait()
        pass_copy(c, mine).wait_send()

    for copy in pending:
        copy.wait_send()


def sds(*shape):
    return jax.ShapeDtypeStruct(shape, BF16)


def buf(*shape):
    return pltpu.VMEM(shape, BF16)


DMA = pltpu.SemaphoreType.DMA


def local(queries, key_rows, value_rows, cotangent, out_weight, patch_counts, destinations):
    smem, hbm, vmem = [pl.BlockSpec(memory_space=space) for space in (pltpu.SMEM, pltpu.HBM, pltpu.VMEM)]
    counts, dests = patch_counts.T, destinations.T
    slots, wt = pl.pallas_call(
        gather_kernel,
        out_shape=(sds(4, SLOT, WIDTH), sds(NDP, FEAT, WIDTH)),
        in_specs=[smem, smem] + [hbm] * 5,
        out_specs=(vmem, hbm),
        scratch_shapes=[
            buf(3, ROWS, WIDTH), buf(DEST, OUT), buf(NDP, FEAT, WIDTH), buf(3, 2, SLOT, WIDTH),
            pltpu.VMEM((DEST, WIDTH), F32), DMA((5,)), DMA((1,)), DMA((31,)), DMA((NDP,)),
        ],
        compiler_params=pltpu.CompilerParams(collective_id=0, has_side_effects=True, vmem_limit_bytes=32 << 20),
        name="gather_forward",
    )(counts, dests, queries, key_rows, value_rows, cotangent, out_weight.T)

    def branch(turn):
        return pl.pallas_call(
            functools.partial(turn_kernel, turn),
            out_shape=sds(4, SLOT, WIDTH),
            in_specs=[vmem],
            out_specs=vmem,
            scratch_shapes=[DMA((4,)), DMA((4,))],
            compiler_params=pltpu.CompilerParams(collective_id=2 + turn, has_side_effects=True),
            name="turn_%d" % turn,
        )

    first = -destinations[0, 0] & (NDP - 1)
    index = jnp.minimum(first, NDP - 1 - first)
    turned = lax.switch(index, [branch(turn) for turn in range(NDP // 2)], slots)

    *outs, grad_weight = pl.pallas_call(
        main_kernel,
        out_shape=(sds(DEST, OUT), sds(ROWS, WIDTH), sds(ROWS, WIDTH), sds(ROWS, WIDTH), sds(FEAT, WIDTH)),
        in_specs=[smem, smem, vmem] + [hbm] * 5,
        out_specs=(hbm,) * 5,
        scratch_shapes=[
            buf(3, ROWS, WIDTH), buf(DEST, OUT), buf(NDP, FEAT, WIDTH), buf(3, 2, SLOT, WIDTH), buf(DEST, WIDTH),
            buf(8, DEST, WIDTH), buf(3, 2, 4, 64, WIDTH), buf(8, 64, WIDTH), buf(8, 64, WIDTH), buf(64, WIDTH),
            buf(8, DEST, WIDTH), buf(2, 4, 4, FEAT, WIDTH), buf(4, 4, FEAT, WIDTH), buf(3, 4, FEAT, WIDTH),
            buf(3, FEAT, WIDTH), buf(3, ROWS, WIDTH), buf(FEAT, WIDTH),
            DMA((5,)), DMA((4,)), DMA((2, 8)), DMA((3, 2, 4)), DMA((3, 2, 4)), DMA((5,)), DMA((5,)),
            DMA((3, 2, 4)), DMA((3, 2, 4)), DMA((8,)), DMA((8,)), DMA((7,)), DMA((7,)),
        ],
        compiler_params=pltpu.CompilerParams(collective_id=1, has_side_effects=True, vmem_limit_bytes=40 << 20),
        name="project_backward",
    )(counts, dests, turned, queries, key_rows, value_rows, cotangent, wt)
    return (*outs, grad_weight.T)


def solution(mesh):
    in_specs = (P("dp", "mp"), P("dp", "mp"), P("dp", "mp"), P("dp", None), P("mp", "dp"), P(), P())
    out_specs = (P("dp", None), P("dp", "mp"), P("dp", "mp"), P("dp", "mp"), P("mp", "dp"))
    return jax.shard_map(local, mesh=mesh, in_specs=in_specs, out_specs=out_specs, check_vma=False)
```

```python
import functools
import math

import jax
import jax.numpy as jnp
from jax import lax
from jax.experimental import pallas as pl
from jax.experimental.pallas import tpu as pltpu
from jax.sharding import PartitionSpec as P

HD = 128
HEADS = 3
NDP = 32
SLOT = 160
ROWS = 320
DEST = 256
FEAT = 96
WIDTH = HEADS * HD
OUT = 3072
SUB = DEST // 2
SCALE = 1.0 / math.sqrt(HD)
MESH = pl.DeviceIdType.MESH
F32 = jnp.float32
BF16 = jnp.bfloat16


def dot(a, b, dims):
    return lax.dot_general(a, b, (dims, ((), ())), preferred_element_type=F32)


def place():
    dp = lax.axis_index("dp")
    mp = lax.axis_index("mp")
    return dp, mp, dp // 8, (dp // 2) % 4, dp % 2, mp // 2, mp % 2


def block(i, size):
    return pl.ds(pl.multiple_of(i * size, size), size)


def dp_of(zh, x, core):
    return (zh * 4 + x) * 2 + core


def mod(a, n):
    return lax.rem(a + n, n)


def remote(src, dst, ss, rs, dp, mp):
    return pltpu.make_async_remote_copy(
        src_ref=src, dst_ref=dst, send_sem=ss, recv_sem=rs, device_id=(dp, mp), device_id_type=MESH
    )


def greet(peers):
    barrier = pltpu.get_barrier_semaphore()
    for dp, mp in peers:
        pl.semaphore_signal(barrier, inc=1, device_id=(dp, mp), device_id_type=MESH)


def greeted(count):
    pl.semaphore_wait(pltpu.get_barrier_semaphore(), count)


def tables(counts_ref, dests_ref, dp):
    first = mod(-dests_ref[0, 0], NDP)
    turn = jnp.minimum(first, NDP - 1 - first)
    swap = (first >= NDP // 2).astype(jnp.int32)
    c0 = counts_ref[0, dp]
    c1 = counts_ref[1, dp]
    home = (
        (jnp.where(swap == 1, c0, 0), jnp.where(swap == 1, c1, c0)),
        (jnp.where(swap == 1, 0, c0), jnp.where(swap == 1, c0, c1)),
    )
    src_a = lax.rem(dp + turn, NDP)
    src_b = mod(dp - turn - 1, NDP)
    count_a = counts_ref[swap, src_a]
    count_b = counts_ref[1 - swap, src_b]
    a_first = src_a < src_b
    dest = (
        (jnp.where(a_first, 0, count_b), count_a),
        (jnp.where(a_first, count_a, 0), count_b),
    )
    return home, dest, turn


def iota(shape, dim):
    return lax.broadcasted_iota(jnp.int32, shape, dim)


def pick(rows, start, count):
    shape = (SLOT, rows)
    r, c = iota(shape, 0), iota(shape, 1)
    return jnp.where((c == r + start) & (r < count), 1.0, 0.0).astype(BF16)


def put(rows, start, count):
    shape = (rows, SLOT)
    r, c = iota(shape, 0), iota(shape, 1)
    return jnp.where((r == c + start) & (c < count), 1.0, 0.0).astype(BF16)


def either(slot, pair):
    return [jnp.where(slot == 0, a, b) for a, b in zip(*pair)]


def probabilities(q, k, count):
    scores = dot(q, k, ((1,), (1,))) * SCALE
    scores = jnp.where(iota(scores.shape, 1) < count, scores, -1e30)
    weights = jnp.exp(scores - jnp.max(scores, axis=-1, keepdims=True))
    return weights / jnp.sum(weights, axis=-1, keepdims=True)


def load_rows(refs, qkv_ref, load, first):
    copies = [pltpu.make_async_copy(ref, qkv_ref.at[i], load.at[first + i]) for i, ref in enumerate(refs)]
    for copy in copies:
        copy.start()
    return copies


def pick_rows(rows_ref, qkv_ref, home):
    @pl.loop(0, 6)
    def _(i):
        picked = pick(ROWS, *either(i % 2, home))
        rows_ref[i // 2, i % 2] = dot(picked, qkv_ref[i // 2], ((1,), (0,))).astype(BF16)


def add(out, *refs):
    @pl.loop(0, out.shape[0] // 32)
    def _(i):
        total = 0.0
        for ref in refs:
            total = total + ref[block(i, 32)].astype(F32)
        out[block(i, 32)] = total.astype(BF16)


def place_rows(ref, parts, spans):
    @pl.loop(0, ref.shape[0] // 64)
    def _(i):
        rows = 0.0
        for part, (start, count) in zip(parts, spans):
            rows = rows + dot(put(64, start - 64 * i, count), part[...], ((1,), (0,)))
        ref[block(i, 64)] = rows.astype(BF16)


def near(i):
    return 2 * i + 1 - 3 * (i // 2)


def jump(i):
    return i + (i + 1) // 3 - 2 * (i // 3)


def fused(
    turn, counts_ref, dests_ref, q_hbm, k_hbm, v_hbm, cot_hbm, w_hbm,
    att_hbm, gq_hbm, gk_hbm, gv_hbm, gw_hbm,
    qkv_ref, cot_ref, wt_ref, rows_ref, slots_ref, turned_ref, dest_ref, sum_ref, part_ref, ring_ref, across_ref,
    fold_ref, att_ref, term_ref, core_ref, xin_ref, zin_ref, grads_ref, gw_ref,
    load, store, att_store, wt_s, wt_r, turn_s, turn_r, ring_s, ring_r, fold_s, fold_r, gath_s, gath_r, pass_s, pass_r,
    red_s, red_r,
):
    dp, mp, zh, x, core, y, zl = place()
    across = y * 2 + 1 - zl
    sibling = dp_of(zh, x, 1 - core)
    back_a, on_a = mod(dp - turn, NDP), lax.rem(dp + turn, NDP)
    on_b, back_b = lax.rem(dp + turn + 1, NDP), mod(dp - turn - 1, NDP)
    routes = [back_a, on_b, on_a, back_b]

    def toward(way):
        return lax.rem(y + 1 + 6 * way, 8) * 2 + zl

    def x_peer(i):
        return dp_of(zh, lax.rem(x + near(i), 4), core)

    def z_peer(i):
        return dp_of(lax.rem(zh + near(i), 4), x, core)

    greet([(dp, toward(0)), (dp, toward(1)), (dp, across), (sibling, mp)])
    greet([(routes[i], mp) for i in range(4) if turn or i % 2])

    @pl.loop(0, 3)
    def _(i):
        greet([(x_peer(i), mp), (z_peer(i), mp)])

    loads = [pltpu.make_async_copy(w_hbm, wt_ref.at[dp], load.at[0]), pltpu.make_async_copy(cot_hbm, cot_ref, load.at[1])]
    loads[0].start()
    loads += load_rows((q_hbm, k_hbm, v_hbm), qkv_ref, load, 2)
    loads[1].start()
    home, dest, _ = tables(counts_ref, dests_ref, dp)

    def shard_copy(i, shard, to):
        return remote(wt_ref.at[shard], wt_ref.at[shard], wt_s.at[i], wt_r.at[shard], to, mp)

    loads[0].wait()
    greeted(14 if turn else 12)

    @pl.loop(0, 3)
    def _(i):
        shard_copy(i, dp, z_peer(i)).start()

    @pl.loop(0, 3)
    def _(i):
        shard_copy(3 + i, dp, x_peer(i)).start()

    shard_copy(6, dp, sibling).start()

    for copy in loads[2:]:
        copy.wait()
    pick_rows(rows_ref, qkv_ref, home)

    @pl.loop(0, 6)
    def _(i):
        slot, cols = i % 2, block(i // 2, HD)
        probs = probabilities(rows_ref[0, slot, :, cols], rows_ref[1, slot, :, cols], either(slot, home)[1])
        slots_ref[slot, :, cols] = dot(probs.astype(BF16), rows_ref[2, slot, :, cols], ((1,), (0,))).astype(BF16)

    def turn_copy(i):
        if turn == 0 and i % 2 == 0:
            return pltpu.make_async_copy(slots_ref.at[i], turned_ref.at[i], turn_s.at[i])
        return remote(slots_ref.at[i], turned_ref.at[i], turn_s.at[i], turn_r.at[i], routes[i], mp)

    turns = [turn_copy(i) for i in range(4)]

    def turn_wait(i):
        if turn == 0 and i % 2 == 0:
            turns[i].wait()
        else:
            turns[i].wait_recv()

    turns[0].start()
    turns[1].start()

    @pl.loop(0, 3)
    def _(i):
        shard = z_peer(i)
        shard_copy(0, shard, dp).wait_recv()

        @pl.loop(0, 3)
        def _(j):
            shard_copy(7 + 4 * i + j, shard, x_peer(j)).start()

        shard_copy(10 + 4 * i, shard, sibling).start()

    @pl.loop(0, 12)
    def _(i):
        shard = dp_of(lax.rem(zh + jump(i // 3), 4), lax.rem(x + near(lax.rem(i, 3)), 4), core)
        shard_copy(0, shard, dp).wait_recv()
        shard_copy(19 + i, shard, sibling).start()

    turn_wait(0)
    turn_wait(1)
    place_rows(dest_ref, [turned_ref.at[0], turned_ref.at[1]], dest)

    @pl.loop(0, 16)
    def _(i):
        shard_copy(0, 2 * i + 1 - core, dp).wait_recv()

    def ring_copy(zone, way, step):
        sem = (zone, way, step)
        src = part_ref.at[zone + zone // 2 * zl, 4 + (2 * way - 1) * step]
        return remote(src, ring_ref.at[sem], ring_s.at[sem], ring_r.at[sem], dp, toward(way))

    def ring_begin(zone):
        first = zone // 2
        ring_copy(zone, first, 0).start()
        ring_copy(zone, 1 - first, 1).start()

    def ring_step(zone, way, step):
        ring_copy(zone, way, step).wait_recv()
        ref = part_ref.at[zone + zone // 2 * zl, 4 + (2 * way - 1) * (step + 1)]
        add(ref, ref, ring_ref.at[zone, way, step])
        ring_copy(zone, way, step + 1).start()

    @pl.loop(0, 8)
    def _(i):
        c = lax.rem(i + 3, 8)
        w = wt_ref[pl.ds(4 * lax.rem(y + c, 8), 4)].reshape(WIDTH, WIDTH)
        part_ref[:, c] = dot(dest_ref[...], w, ((1,), (1,))).astype(BF16).reshape(4, 64, WIDTH)

    def share_copy(i):
        lo, hi = ((3, 6), (0, 3), (6, 8))[i]
        span = pl.ds(lo, hi - lo)
        return remote(part_ref.at[3 - zl, span], across_ref.at[span], fold_s.at[i], fold_r.at[i], dp, across), lo, hi

    def share_take(i):
        copy, lo, hi = share_copy(i)
        copy.wait_recv()

        @pl.loop(lo, hi)
        def _(c):
            add(part_ref.at[2 + zl, c], part_ref.at[2 + zl, c], across_ref.at[c])

    pl.loop(0, 2)(ring_begin)
    for i in range(3):
        share_copy(i)[0].start()

    loads[1].wait()
    sum_ref[...] = jnp.zeros_like(sum_ref)

    @pl.loop(0, 8)
    def _(c):
        w = wt_ref[pl.ds(4 * c, 4)].reshape(WIDTH, WIDTH)
        sum_ref[...] += dot(cot_ref[:, block(c, WIDTH)], w, ((1,), (0,)))

    @pl.loop(0, 2)
    def _(slot):
        picked = pick(DEST, *either(slot, dest))
        slots_ref[2 + slot] = dot(picked, sum_ref[...].astype(BF16), ((1,), (0,))).astype(BF16)

    turns[2].start()
    turns[3].start()

    @pl.loop(0, 8)
    def _(c):
        term = dot(cot_ref[:, block(c, WIDTH)], dest_ref[...], ((0,), (0,))).astype(BF16)
        for i in range(4):
            term_ref[i % 2, lax.rem(2 * c + i // 2, 4), c // 2] = term[i * FEAT : (i + 1) * FEAT]

    swap = remote(term_ref.at[1 - core], core_ref, red_s.at[0], red_r.at[0], sibling, mp)
    swap.start()

    @pl.loop(0, 2)
    def _(zone):
        ring_step(zone, 0, 0)

    share_take(0)
    ring_begin(2)
    swap.wait_recv()

    @pl.loop(0, 16)
    def _(i):
        ref = term_ref.at[core, i // 4, lax.rem(i, 4)]
        add(ref, ref, core_ref.at[i // 4, lax.rem(i, 4)])

    def x_copy(n):
        src = term_ref.at[core, lax.rem(x + near(n), 4)]
        return remote(src, xin_ref.at[n], red_s.at[1 + n], red_r.at[1 + n], x_peer(n), mp)

    def z_copy(n):
        src = term_ref.at[core, x, lax.rem(zh + near(n), 4)]
        return remote(src, zin_ref.at[n], red_s.at[4 + n], red_r.at[4 + n], z_peer(n), mp)

    @pl.loop(0, 3)
    def _(n):
        x_copy(n).start()

    def ring_pair(step):
        @pl.loop(0, 4)
        def _(i):
            ring_step(lax.rem(i, 2), 1 - i // 2, step)

    def ring_end(zone):
        ring_copy(zone, 0, 3).wait_recv()
        ring_copy(zone, 1, 3).wait_recv()
        own = part_ref.at[zone + zone // 2 * zl, 0]
        add(own, own, ring_ref.at[zone, 0, 3], ring_ref.at[zone, 1, 3])

    ring_pair(1)
    ring_step(2, 1, 0)
    ring_pair(2)
    share_take(1)
    share_take(2)
    ring_step(2, 1, 1)
    ring_step(2, 0, 1)
    pl.loop(0, 2)(ring_end)
    fold = remote(part_ref.at[1 - zl, 0], fold_ref, fold_s.at[3], fold_r.at[3], dp, across)
    fold.start()
    ring_step(2, 1, 2)
    ring_step(2, 0, 2)

    def low_copy(quarter):
        return remote(att_ref.at[quarter, 0], att_ref.at[quarter, 0], fold_s.at[4], fold_r.at[4], dp, across)

    def att_copy(quarter, c):
        rows, cols = block(quarter, 64), block(lax.rem(y + c, 8), WIDTH)
        return pltpu.make_async_copy(att_ref.at[quarter, c], att_hbm.at[rows, cols], att_store.at[quarter, c])

    def quarter_of(zone):
        return (zone + 2) * (1 - zone // 2) + zone // 2 * zl

    def gather_copy(zone, way, step):
        quarter, sem = quarter_of(zone), (zone, way, step)
        src, dst = lax.rem(8 + (2 * way - 1) * step, 8), lax.rem(8 + (2 * way - 1) * (step + 1), 8)
        return remote(
            att_ref.at[quarter, src], att_ref.at[quarter, dst], gath_s.at[sem], gath_r.at[sem], dp, toward(way)
        )

    def gather_begin(zone):
        gather_copy(zone, 0, 0).start()
        gather_copy(zone, 1, 0).start()
        att_copy(quarter_of(zone), 0).start()

    def pass_copy(c, quarter):
        return remote(att_ref.at[quarter, c], att_ref.at[quarter, c], pass_s.at[c], pass_r.at[c], dp, across)

    fold.wait_recv()
    add(att_ref.at[zl, 0], part_ref.at[zl, 0], fold_ref)
    gather_begin(2)
    pass_copy(0, zl).start()
    ring_end(2)
    att_ref[2 + zl, 0] = part_ref[2 + zl, 0]
    low_copy(2 + zl).start()

    def gather_step(zone, way, step, more):
        gather_copy(zone, way, step).wait_recv()
        if more:
            gather_copy(zone, way, step + 1).start()
        c = lax.rem(8 + (2 * way - 1) * (step + 1), 8)
        att_copy(quarter_of(zone), c).start()
        if isinstance(zone, int):
            pass_copy(c, zl).start()

    def gather_pair(step, ways, more):
        @pl.loop(0, 2 * ways)
        def _(i):
            gather_step(lax.rem(i, 2), i // 2, step, more)

    gather_step(2, 1, 0, True)
    gather_step(2, 0, 0, True)
    low_copy(3 - zl).wait_recv()
    pl.loop(0, 2)(gather_begin)

    turn_wait(2)
    turn_wait(3)

    @pl.loop(0, 6)
    def _(i):
        slot, cols = i % 2, block(i // 2, HD)
        q, k, v = rows_ref[0, slot, :, cols], rows_ref[1, slot, :, cols], rows_ref[2, slot, :, cols]
        gm = turned_ref[2 + slot, :, cols]
        probs = probabilities(q, k, either(slot, home)[1])
        gp = dot(gm, v, ((1,), (1,)))
        inner = jnp.sum(gp * probs, axis=-1, keepdims=True)
        gs = (probs * (gp - inner) * SCALE).astype(BF16)
        rows_ref[0, slot, :, cols] = dot(gs, k, ((1,), (0,))).astype(BF16)
        rows_ref[1, slot, :, cols] = dot(gs, q, ((0,), (0,))).astype(BF16)
        rows_ref[2, slot, :, cols] = dot(probs.astype(BF16), gm, ((0,), (0,))).astype(BF16)

    @pl.loop(0, 3)
    def _(n):
        x_copy(n).wait_recv()

    @pl.loop(0, 4)
    def _(i):
        add(term_ref.at[core, x, i], term_ref.at[core, x, i], *[xin_ref.at[n, i] for n in range(3)])

    @pl.loop(0, 3)
    def _(n):
        z_copy(n).start()

    gather_step(2, 1, 1, True)
    gather_step(2, 0, 1, True)
    gather_pair(0, 2, True)

    @pl.loop(0, 3)
    def _(i):
        place_rows(grads_ref.at[i], [rows_ref.at[i, 0], rows_ref.at[i, 1]], home)

    gather_step(2, 1, 2, True)
    gather_step(2, 0, 2, False)
    gather_pair(1, 2, True)
    gather_step(2, 1, 3, False)
    gather_pair(2, 1, True)

    @pl.loop(0, 2)
    def _(zone):
        gather_step(zone, 1, 2, False)

    outs = [pltpu.make_async_copy(grads_ref.at[i], ref, store.at[i]) for i, ref in enumerate((gq_hbm, gk_hbm, gv_hbm))]
    outs.append(pltpu.make_async_copy(gw_ref, gw_hbm, store.at[3]))

    @pl.loop(0, 3)
    def _(n):
        z_copy(n).wait_recv()

    add(gw_ref, term_ref.at[core, x, zh], *[zin_ref.at[n] for n in range(3)])
    for copy in outs:
        copy.start()
    gather_pair(3, 1, False)

    @pl.loop(0, 8)
    def _(c):
        pass_copy(c, 1 - zl).wait_recv()
        att_copy(1 - zl, c).start()

    @pl.loop(0, 31)
    def _(i):
        shard_copy(i, dp, sibling).wait_send()

    for i in range(4):
        if turn or i % 2:
            turns[i].wait_send()
    for copy in (swap, fold, low_copy(2 + zl), *[share_copy(i)[0] for i in range(3)]):
        copy.wait_send()

    @pl.loop(0, 3)
    def _(n):
        x_copy(n).wait_send()
        z_copy(n).wait_send()

    @pl.loop(0, 6)
    def _(i):
        zone, way = lax.rem(i, 3), i // 3

        @pl.loop(0, 4)
        def _(step):
            @pl.when((step > 0) | (way == zone // 2))
            def _():
                ring_copy(zone, way, step).wait_send()

            @pl.when((step < 3) | (way == zone // 2))
            def _():
                gather_copy(zone, way, step).wait_send()

    @pl.loop(0, 8)
    def _(c):
        pass_copy(c, zl).wait_send()
        for quarter in range(4):
            att_copy(quarter, c).wait()

    for copy in outs:
        copy.wait()


def hand_over(*refs):
    sems, count = refs[-1], len(refs) // 2
    copies = [pltpu.make_async_copy(refs[i], refs[count + i], sems.at[i]) for i in range(count)]
    for copy in copies:
        copy.start()
    for copy in copies:
        copy.wait()


def sds(*shape):
    return jax.ShapeDtypeStruct(shape, BF16)


def buf(*shape):
    return pltpu.VMEM(shape, BF16)


DMA = pltpu.SemaphoreType.DMA


def local(queries, key_rows, value_rows, cotangent, out_weight, patch_counts, destinations):
    smem, hbm = pl.BlockSpec(memory_space=pltpu.SMEM), pl.BlockSpec(memory_space=pl.ANY)

    def branch(turn):
        return pl.pallas_call(
            functools.partial(fused, turn),
            out_shape=(sds(DEST, OUT), sds(ROWS, WIDTH), sds(ROWS, WIDTH), sds(ROWS, WIDTH), sds(FEAT, WIDTH)),
            in_specs=[smem, smem] + [hbm] * 5,
            out_specs=(hbm,) * 5,
            scratch_shapes=[
                buf(3, ROWS, WIDTH), buf(DEST, OUT), buf(NDP, FEAT, WIDTH), buf(3, 2, SLOT, WIDTH), buf(4, SLOT, WIDTH),
                buf(4, SLOT, WIDTH), buf(DEST, WIDTH), pltpu.VMEM((DEST, WIDTH), F32), buf(4, 8, 64, WIDTH),
                buf(3, 2, 4, 64, WIDTH), buf(8, 64, WIDTH), buf(64, WIDTH), buf(4, 8, 64, WIDTH),
                buf(2, 4, 4, FEAT, WIDTH), buf(4, 4, FEAT, WIDTH), buf(3, 4, FEAT, WIDTH), buf(3, FEAT, WIDTH),
                buf(3, ROWS, WIDTH), buf(FEAT, WIDTH),
                DMA((5,)), DMA((4,)), DMA((4, 8)), DMA((31,)), DMA((NDP,)), DMA((4,)), DMA((4,)),
                DMA((3, 2, 4)), DMA((3, 2, 4)), DMA((5,)), DMA((5,)), DMA((3, 2, 4)), DMA((3, 2, 4)),
                DMA((8,)), DMA((8,)), DMA((7,)), DMA((7,)),
            ],
            compiler_params=pltpu.CompilerParams(
                collective_id=turn, has_side_effects=True, vmem_limit_bytes=48 << 20
            ),
            name="layer_turn_%d" % turn,
        )

    first = -destinations[0, 0] & (NDP - 1)
    index = jnp.minimum(first, NDP - 1 - first)
    results = lax.switch(
        index,
        [branch(turn) for turn in range(NDP // 2)],
        patch_counts.T, destinations.T, queries, key_rows, value_rows, cotangent, out_weight.T,
    )
    *outs, grad_weight = pl.pallas_call(
        hand_over,
        out_shape=tuple(sds(*result.shape) for result in results),
        in_specs=[hbm] * 5,
        out_specs=(hbm,) * 5,
        scratch_shapes=[DMA((5,))],
        name="hand_over",
    )(*results)
    return (*outs, grad_weight.T)


def solution(mesh):
    in_specs = (P("dp", "mp"), P("dp", "mp"), P("dp", "mp"), P("dp", None), P("mp", "dp"), P(), P())
    out_specs = (P("dp", None), P("dp", "mp"), P("dp", "mp"), P("dp", "mp"), P("mp", "dp"))
    return jax.shard_map(local, mesh=mesh, in_specs=in_specs, out_specs=out_specs, check_vma=False)
```
